32 devices in a mesh: seq: 8 (over z, x), tp: 4 (over y, core).
Axes of the slice: x: 2, y: 2, z: 4, core: 2. Of those that a mesh axis runs over, the one named last changes fastest.
Arguments:
- layer_in: bfloat16 [2, 2048, 2, 512], P(None, 'seq'), may hold values from -6 to 6
- cotangent: bfloat16 [2, 2048, 2, 512], P(None, 'seq'), may hold values from -6 to 6
- clip_of_frame: int32 [2, 2], replicated, may hold values from 0 to 1, as said below
- w_query: bfloat16 [2, 512, 512], P(None, None, 'tp'), may hold values from -0.375 to 0.375
- w_key: bfloat16 [2, 512, 512], P(None, None, 'tp'), may hold values from -0.375 to 0.375
- w_value: bfloat16 [2, 512, 512], P(None, None, 'tp'), may hold values from -0.25 to 0.25
- w_out: bfloat16 [2, 512, 512], P(None, 'tp'), may hold values from -1.796875 to 1.796875
- w_up: bfloat16 [2, 512, 2048], P(None, None, 'tp'), may hold values from -0.25 to 0.25
- w_down: bfloat16 [2, 2048, 512], P(None, 'tp'), may hold values from -0.125 to 0.125
- norm1_gain: float32 [2, 512], replicated, may hold values from 0.5 to 1.5
- norm1_bias: float32 [2, 512], replicated, may hold values from -3 to 3
- norm2_gain: float32 [2, 512], replicated, may hold values from 0.5 to 1.5
- norm2_bias: float32 [2, 512], replicated, may hold values from -3 to 3
Outputs:
- layer_out: bfloat16 [2, 2048, 2, 512], P(None, 'seq')
- input_grad: bfloat16 [2, 2048, 2, 512], P(None, 'seq')
- grad_query: float32 [2, 512, 512], P(None, None, 'tp')
- grad_key: float32 [2, 512, 512], P(None, None, 'tp')
- grad_value: float32 [2, 512, 512], P(None, None, 'tp')
- grad_out: float32 [2, 512, 512], P(None, 'tp')
- grad_up: float32 [2, 512, 2048], P(None, None, 'tp')
- grad_down: float32 [2, 2048, 512], P(None, 'tp')
- grad_gain1: float32 [2, 512], replicated
- grad_bias1: float32 [2, 512], replicated
- grad_gain2: float32 [2, 512], replicated
- grad_bias2: float32 [2, 512], replicated
The draws below stay inside these ranges and needn't reach their ends.
Inputs may be any that keep to these rules, and one draw needn't show every extreme that they name: `clip_of_frame`: in each stream clip numbers never fall; frames with equal numbers form one clip, and a clip's number is the index of its first frame. The last frame of one stream always starts a clip of its own; in the other stream, chosen from the seed, all 2 frames form a single clip.
All inputs are finite; a program needn't handle non-finite values.
Results may differ from the reference program's by a relative error of at most 0.024.
Values may be sent and summed in bfloat16 or wider, within the bound.
No kernel may reach another device: no remote copies, remote signals or barrier semaphores. Data moves between devices by JAX's collectives and lax.ppermute only.
A program may use at most 256 MiB of HBM per device.

```python
import math
from functools import partial
import jax
import jax.numpy as jnp
from jax import lax

D = 512
HEADS = 8
HEAD_DIM = 64
FF = 2048
NETS = 2
STREAMS = 2
FRAME = 1024
SLEN = 2048
FRAMES = 2


def draw_clip_of_frame(key, part):
    key = jax.random.fold_in(key, 11)
    cut_key, pick_key = jax.random.split(key)
    cuts = jax.random.randint(cut_key, (STREAMS, FRAMES), 0, 2)
    whole = jax.random.randint(pick_key, (), 0, STREAMS)
    frame = jnp.arange(FRAMES, dtype=jnp.int32)[None, :]
    stream = jnp.arange(STREAMS, dtype=jnp.int32)[:, None]
    cuts = jnp.where(frame == FRAMES - 1, 1, cuts)
    cuts = jnp.where(frame == 0, 1, cuts)
    cuts = jnp.where((stream == whole) & (frame > 0), 0, cuts)
    starts = jnp.where(cuts > 0, frame, 0)
    return lax.cummax(starts, axis=1).astype(jnp.int32)


def shard_levels(rng, shape, pieces, low, largest):
    level, own = 1.0, jax.random.fold_in(rng, 6)
    for dim, shards_of in pieces:
        steps = jnp.exp(jax.random.uniform(jax.random.fold_in(own, dim), (shards_of,), jnp.float32, low / len(pieces), largest / len(pieces)))
        level = level * jnp.repeat(steps, shape[dim] // shards_of).reshape([-1 if axis == dim else 1 for axis in range(len(shape))])
    return level


def bell_draw(rng, dims, scale, limit, cuts=(), held_as=jnp.bfloat16):
    result = jax.random.normal(rng, dims, jnp.float32) * scale
    if len(cuts) > 0:
        result = shard_levels(rng, dims, cuts, -0.22, 0.18) * result
    return jnp.clip(result, min=-limit, max=limit).astype(held_as)


def setup_inputs(seed: int = 0) -> dict:
    seeds = jax.random.split(jax.random.key(seed), 14)
    layer_in = bell_draw(seeds[0], (NETS, SLEN, STREAMS, D), 1.0, 6.0, ((1, 8),))
    cotangent = bell_draw(seeds[1], (NETS, SLEN, STREAMS, D), 1.0, 6.0, ((1, 8),))
    clip_of_frame = draw_clip_of_frame(jax.random.fold_in(seeds[13], 71), 0)
    w_query = bell_draw(seeds[3], (NETS, D, D), (D // 2) ** -0.5, 0.375, ((2, 4),))
    w_key = bell_draw(seeds[4], (NETS, D, D), (D // 2) ** -0.5, 0.375, ((2, 4),))
    w_value = bell_draw(seeds[5], (NETS, D, D), D ** -0.5, 0.25, ((2, 4),))
    w_out = bell_draw(seeds[6], (NETS, D, D), 0.3, 1.796875, ((1, 4),))
    w_up = bell_draw(seeds[7], (NETS, D, FF), D ** -0.5, 0.25, ((2, 4),))
    w_down = bell_draw(seeds[8], (NETS, FF, D), FF ** -0.5, 0.125, ((1, 4),))
    norm1_gain = jnp.clip(1.0 + 0.1 * jax.random.normal(seeds[9], (NETS, D), jnp.float32), 0.5, 1.5)
    norm1_bias = bell_draw(seeds[10], (NETS, D), 0.5, 3.0, (), jnp.float32)
    norm2_gain = jnp.clip(1.0 + 0.1 * jax.random.normal(seeds[11], (NETS, D), jnp.float32), 0.5, 1.5)
    norm2_bias = bell_draw(seeds[12], (NETS, D), 0.5, 3.0, (), jnp.float32)
    return {"layer_in": layer_in, "cotangent": cotangent, "clip_of_frame": clip_of_frame, "w_query": w_query, "w_key": w_key, "w_value": w_value, "w_out": w_out, "w_up": w_up, "w_down": w_down, "norm1_gain": norm1_gain, "norm1_bias": norm1_bias, "norm2_gain": norm2_gain, "norm2_bias": norm2_bias}


@jax.custom_vjp
def low(v):
    return lax.optimization_barrier(v.astype(jnp.bfloat16)).astype(jnp.float32)

@jax.custom_vjp
def low_back(v):
    return v

def low_keep(v):
    return (low(v), None)

def low_pass(kept, grad):
    return (grad,)

def back_keep(v):
    return (v, None)

def back_low(kept, grad):
    return (low(grad),)
low.defvjp(low_keep, low_pass)
low_back.defvjp(back_keep, back_low)

def layer_norm(inputs, gain, bias):
    center = inputs - lax.optimization_barrier(jnp.mean(inputs, axis=-1, keepdims=True))
    spread = lax.optimization_barrier(jnp.mean(center * center, axis=-1, keepdims=True))
    return center * lax.rsqrt(spread + 1e-05) * gain + bias

def project(inputs, weight):
    return jnp.einsum('lsd,dc->lsc', inputs, weight, precision=lax.Precision.HIGHEST)

def attend(queries, keys, values, clip_table):
    length, streams, features = queries.shape
    row_block = math.gcd(length, 512)
    score_scale = 1.0 / math.sqrt(HEAD_DIM)
    positions = jnp.arange(length, dtype=jnp.int32)
    results = []
    for stream in range(streams):
        clip_ids = clip_table[stream][positions // FRAME]
        query_rows = queries[:, stream].reshape(length // row_block, row_block, HEADS, HEAD_DIM)
        key_rows = keys[:, stream].reshape(length, HEADS, HEAD_DIM)
        value_rows = values[:, stream].reshape(length, HEADS, HEAD_DIM)
        query_ids = clip_ids.reshape(length // row_block, row_block)

        def one_block(block_args, key_rows=key_rows, value_rows=value_rows, clip_ids=clip_ids):
            query_block, block_ids = block_args
            scores = jnp.einsum('qhe,khe->hqk', query_block, key_rows, precision=lax.Precision.HIGHEST) * score_scale
            scores = low_back(scores)
            same_clip = block_ids[:, None] == clip_ids[None, :]
            scores = jnp.where(same_clip[None], scores, -1e+30)
            probs = jax.nn.softmax(scores, axis=-1)
            return jnp.einsum('hqk,khe->qhe', low(probs), value_rows, precision=lax.Precision.HIGHEST)
        blocks_out = lax.map(jax.checkpoint(one_block), (query_rows, query_ids))
        results.append(blocks_out.reshape(length, features))
    return jnp.stack(results, axis=1)

def layer_pass(inputs, wq_in, wk_in, wv_in, wo_in, wu_in, wd_in, gain_one, bias_one, gain_two, bias_two, clip_table):
    normed = low(layer_norm(inputs, gain_one, bias_one))
    queries = low_back(low(project(normed, wq_in)))
    keys = low_back(low(project(normed, wk_in)))
    values = low_back(low(project(normed, wv_in)))
    attended = low_back(low(attend(queries, keys, values, clip_table)))
    middle = inputs + low_back(project(attended, wo_in))
    second = low(layer_norm(middle, gain_two, bias_two))
    hidden_pre = low_back(project(second, wu_in))
    hidden = low(jax.nn.gelu(hidden_pre, approximate=True))
    return middle + low_back(project(hidden, wd_in))

def reference(layer_in, cotangent, clip_of_frame, w_query, w_key, w_value, w_out, w_up, w_down, norm1_gain, norm1_bias, norm2_gain, norm2_bias):
    results = []
    input_grads = []
    weight_grads = []
    for net_index in range(2):
        inputs = layer_in[net_index].astype(jnp.float32)
        output, pullback = jax.vjp(partial(layer_pass, clip_table=clip_of_frame), inputs, w_query[net_index].astype(jnp.float32), w_key[net_index].astype(jnp.float32), w_value[net_index].astype(jnp.float32), w_out[net_index].astype(jnp.float32), w_up[net_index].astype(jnp.float32), w_down[net_index].astype(jnp.float32), norm1_gain[net_index].astype(jnp.float32), norm1_bias[net_index].astype(jnp.float32), norm2_gain[net_index].astype(jnp.float32), norm2_bias[net_index].astype(jnp.float32))
        gradients = pullback(cotangent[net_index].astype(jnp.float32))
        results.append(output.astype(jnp.bfloat16))
        input_grads.append(gradients[0].astype(jnp.bfloat16))
        weight_grads.append(gradients[1:])
    stacked = [jnp.stack([weight_grads[0][slot], weight_grads[1][slot]], axis=0).astype(jnp.float32) for slot in range(10)]
    return (jnp.stack(results, axis=0), jnp.stack(input_grads, axis=0), stacked[0], stacked[1], stacked[2], stacked[3], stacked[4], stacked[5], stacked[6], stacked[7], stacked[8], stacked[9])
```

```python
import math

import jax
import jax.numpy as jnp
from jax import lax
from jax.experimental import pallas as pl
from jax.experimental.pallas import tpu as pltpu
from jax.sharding import PartitionSpec as P

HEAD_DIM = 64
EPS = 1e-05
BF = jnp.bfloat16
F32 = jnp.float32
VMEM_LIMIT = 50 * 1024 * 1024
GROUP = 4
PIECES = 8
ORDER = (0, 1, 2)
RUP, RDOWN, ROUT = 64, 64, 16
C_GELU = math.sqrt(2.0 / math.pi)


def dot(a, b, ca=1, cb=0):
    return lax.dot_general(a, b, (((ca,), (cb,)), ((), ())), preferred_element_type=F32)


def place(value):
    out = 0
    for rank, bit in enumerate(ORDER):
        out = out + ((value >> bit) & 1) * (1 << (2 - rank))
    return out


def norm_parts(v):
    center = v - jnp.mean(v, axis=-1, keepdims=True)
    inv = lax.rsqrt(jnp.mean(center * center, axis=-1, keepdims=True) + EPS)
    return center * inv, inv


def norm_back(dout, hat, inv, gain):
    e = dout * gain
    mean_e = jnp.mean(e, axis=-1, keepdims=True)
    mean_eh = jnp.mean(e * hat, axis=-1, keepdims=True)
    return (e - mean_e - hat * mean_eh) * inv


def vspec():
    return pl.BlockSpec(memory_space=pltpu.VMEM)


def sspec():
    return pl.BlockSpec(memory_space=pltpu.SMEM)


def call(kernel, outs, scalars, args, scratch=(), flops=0, nbytes=0, trans=0):
    return pl.pallas_call(
        kernel,
        out_shape=[jax.ShapeDtypeStruct(s, d) for s, d in outs],
        in_specs=[sspec()] + [vspec()] * len(args),
        out_specs=[vspec()] * len(outs),
        scratch_shapes=list(scratch),
        compiler_params=pltpu.CompilerParams(vmem_limit_bytes=VMEM_LIMIT),
        cost_estimate=pl.CostEstimate(flops=flops, bytes_accessed=nbytes, transcendentals=trans),
    )(scalars, *args)


def pick(sc, refs, scratch):
    for e in range(4):
        @pl.when(sc[0] == e)
        def _(e=e):
            scratch[...] = refs[e][...]


def project_kernel(sc, x0, x1, x2, x3, wo, wy, wc, gain, bias, qkv, w_s):
    pick(sc, (wo, wc.at[0], wy, wc.at[1]), w_s)
    g = gain[pl.ds(sc[1], 1), :]
    b = bias[pl.ds(sc[1], 1), :]
    for k, ref in enumerate((x0, x1, x2, x3)):
        hat, _ = norm_parts(ref[...].astype(F32))
        a = (hat * g + b).astype(BF)
        out = dot(a, w_s[...])
        rows = pl.ds(k * ref.shape[0], ref.shape[0])
        qkv[rows, 0:128] = (out[:, 0:128].astype(BF).astype(F32) * (1.0 / math.sqrt(HEAD_DIM))).astype(BF)
        qkv[rows, 128:384] = out[:, 128:384].astype(BF)


def attend_kernel(frames, qb, act, qkv, kvx, o_out, ot_out, lse_out, qm, vt, m_s, l_s, acc):
    n = qkv.shape[0]
    lane = lax.broadcasted_iota(jnp.int32, (n, 128), 1)
    q = qkv[:, 0:128]
    qm[0] = jnp.where(lane < HEAD_DIM, q, jnp.zeros_like(q))
    qm[1] = jnp.where(lane < HEAD_DIM, jnp.zeros_like(q), q)

    def frame_step(k, v, first):
        vt[...] = v.T
        for h in range(2):
            def block(b, _, h=h):
                cols = pl.ds(pl.multiple_of(b * qb, qb), qb)
                st = dot(k, qm[h, cols, :], 1, 1)
                top = jnp.max(st, axis=0, keepdims=True)
                if first:
                    m = top
                else:
                    old = m_s[h:h + 1, cols]
                    m = jnp.maximum(old, top)
                pt = jnp.exp(st - m)
                total = jnp.sum(pt, axis=0, keepdims=True)
                new = dot(vt[h * HEAD_DIM:(h + 1) * HEAD_DIM, :], pt.astype(BF))
                rows = slice(h * HEAD_DIM, (h + 1) * HEAD_DIM)
                if not first:
                    fix = jnp.exp(old - m)
                    total = total + l_s[h:h + 1, cols] * fix
                    new = new + acc[rows, cols] * fix
                m_s[h:h + 1, cols] = m
                l_s[h:h + 1, cols] = total
                acc[rows, cols] = new
                return 0

            lax.fori_loop(0, n // qb, block, 0)

    frame_step(qkv[:, 128:256], qkv[:, 256:384], True)
    for r in range(frames - 1):
        @pl.when(act[r + 1] != 0)
        def _(r=r):
            frame_step(kvx[r, :, 0:128], kvx[r, :, 128:256], False)

    for h in range(2):
        rows = slice(h * HEAD_DIM, (h + 1) * HEAD_DIM)
        ot_out[rows, :] = acc[rows, :] / l_s[h:h + 1, :]
        lse_out[h:h + 1, :] = m_s[h:h + 1, :] + jnp.log(l_s[h:h + 1, :])
    o_out[...] = ot_out[...].T.astype(BF)


def attend_back_kernel(frames, qb, act, qkv, kvx, do, ot, lse, dq_out, dkv_own, dkv_x, qm, dom, kt, delta, dqt, dk_s, dv_s):
    n = qkv.shape[0]
    lane = lax.broadcasted_iota(jnp.int32, (n, 128), 1)
    q = qkv[:, 0:128]
    d = do[...]
    zero = jnp.zeros_like(q)
    qm[0] = jnp.where(lane < HEAD_DIM, q, zero)
    qm[1] = jnp.where(lane < HEAD_DIM, zero, q)
    dom[0] = jnp.where(lane < HEAD_DIM, d, zero)
    dom[1] = jnp.where(lane < HEAD_DIM, zero, d)
    dt = d.astype(F32).T * ot[...]
    for h in range(2):
        delta[h:h + 1, :] = jnp.sum(dt[h * HEAD_DIM:(h + 1) * HEAD_DIM, :], axis=0, keepdims=True)
    dqt[...] = jnp.zeros_like(dqt)

    def frame_step(k, v):
        kt[...] = k.T
        dk_s[...] = jnp.zeros_like(dk_s)
        dv_s[...] = jnp.zeros_like(dv_s)
        for h in range(2):
            def block(b, _, h=h):
                cols = pl.ds(pl.multiple_of(b * qb, qb), qb)
                qh = qm[h, cols, :]
                dh = dom[h, cols, :]
                pt = jnp.exp(dot(k, qh, 1, 1) - lse[h:h + 1, cols])
                dv_s[...] += dot(pt.astype(BF), dh)
                dst = (pt * (dot(v, dh, 1, 1) - delta[h:h + 1, cols])).astype(BF)
                dk_s[...] += dot(dst, qh)
                rows = slice(h * HEAD_DIM, (h + 1) * HEAD_DIM)
                dqt[rows, cols] += dot(kt[rows, :], dst)
                return 0

            lax.fori_loop(0, n // qb, block, 0)

    for r in range(frames - 1):
        @pl.when(act[r + 1] != 0)
        def _(r=r):
            frame_step(kvx[r, :, 0:128], kvx[r, :, 128:256])
            dkv_x[r, :, 0:128] = dk_s[...].astype(BF)
            dkv_x[r, :, 128:256] = dv_s[...].astype(BF)

        @pl.when(act[r + 1] == 0)
        def _(r=r):
            dkv_x[r] = jnp.zeros_like(dkv_x[r])

    frame_step(qkv[:, 128:256], qkv[:, 256:384])
    dkv_own[:, 0:128] = dk_s[...]
    dkv_own[:, 128:256] = dv_s[...]
    dq_out[...] = (dqt[...].T * (1.0 / math.sqrt(HEAD_DIM))).astype(BF)


def gelu_parts(u):
    t = jnp.tanh(C_GELU * (u + 0.044715 * (u * u * u)))
    value = 0.5 * u * (1.0 + t)
    slope = 0.5 * (1.0 + t) + 0.5 * u * (1.0 - t * t) * (C_GELU * (1.0 + 3 * 0.044715 * (u * u)))
    return value, slope


def middle_kernel(sc, x, g, o0, o1, o2, o3, wo, wy, wc, gain, bias, do_out, lout, h_out, du_out, b_out, dz_out, dy_out, gains, wo_s):
    mats = (wo, wc.at[0], wy, wc.at[1])
    for e in range(4):
        wo_s[e] = mats[e][1024:1152, :]
    gain_row = gain[pl.ds(sc[1], 1), :]
    mid = x[...].astype(F32)
    for k, ref in enumerate((o0, o1, o2, o3)):
        mid = mid + dot(ref[...], wo_s[sc[0] ^ k])
    hat, inv = norm_parts(mid)
    b = (hat * gain_row + bias[pl.ds(sc[1], 1), :]).astype(BF)
    b_out[...] = b
    cot = g[...]
    dy_out[...] = mid
    db = jnp.zeros_like(mid)
    for e in range(4):
        up = mats[e][0:512, :]
        down = mats[e][512:1024, :]
        value, slope = gelu_parts(dot(b, up))
        h = value.astype(BF)
        h_out[:, e * 512:(e + 1) * 512] = h
        dy_out[...] += dot(h, down)
        du = (dot(cot, down, 1, 1) * slope).astype(BF)
        du_out[:, e * 512:(e + 1) * 512] = du
        db = db + dot(du, up, 1, 1)
    lout[...] = dy_out[...].astype(BF)
    gains[0:1, :] = jnp.sum(db * hat, axis=0, keepdims=True)
    gains[1:2, :] = jnp.sum(db, axis=0, keepdims=True)
    dy = cot.astype(F32) + norm_back(db, hat, inv, gain_row)
    dy_out[...] = dy
    dz = dy.astype(BF)
    dz_out[...] = dz
    for k in range(4):
        do_out[k] = dot(dz, wo_s[sc[0] ^ k], 1, 1).astype(BF)


def store_pieces(dst, e, row, value, rows, sc):
    for a in range(PIECES):
        dst[place(a) ^ sc[2], e, row:row + rows, :] = value[a * rows:(a + 1) * rows, :]


def middle_grads_kernel(shards, sc, h, du, b, dz, g, o0, o1, o2, o3, out, o_s):
    for k, ref in enumerate((o0, o1, o2, o3)):
        o_s[k] = ref[...]
    for slot, e in enumerate(shards):
        cols = slice(e * 512, (e + 1) * 512)
        store_pieces(out, slot, 0, dot(b[...], du[:, cols], 0, 0).astype(BF), RUP, sc)
        store_pieces(out, slot, RUP, dot(h[:, cols], g[...], 0, 0).astype(BF), RDOWN, sc)
        store_pieces(out, slot, RUP + RDOWN, dot(o_s[sc[0] ^ e], dz[...], 0, 0).astype(BF), ROUT, sc)


def input_kernel(sc, x, dy, d0, d1, d2, d3, wo, wy, wc, gain, bias, gin, gains, keep, send, w_s, d_s):
    mats = (wo, wc.at[0], wy, wc.at[1])
    for e in range(4):
        w_s[e] = mats[e][...]
    gain_row = gain[pl.ds(sc[1], 1), :]
    hat, inv = norm_parts(x[...].astype(F32))
    a = (hat * gain_row + bias[pl.ds(sc[1], 1), :]).astype(BF)
    da = jnp.zeros_like(hat)
    for k, ref in enumerate((d0, d1, d2, d3)):
        d_s[k] = ref[...]
        da = da + dot(ref[...], w_s[sc[0] ^ k], 1, 1)
    gains[0:1, :] = jnp.sum(da * hat, axis=0, keepdims=True)
    gains[1:2, :] = jnp.sum(da, axis=0, keepdims=True)
    gin[...] = (dy[...] + norm_back(da, hat, inv, gain_row)).astype(BF)
    for e in range(4):
        dst = (keep, send)[e % 2]
        store_pieces(dst, e // 2, 0, dot(a, d_s[sc[0] ^ e], 0, 0).astype(BF), 64, sc)


def unpack_kernel(sc, one, two, up, down, out, q, k, v):
    for rel in range(2):
        net = sc[1] ^ rel
        for spot in range(PIECES):
            piece = sc[2] ^ spot
            a = 0
            for rank, bit in enumerate(ORDER):
                a = a + ((piece >> (2 - rank)) & 1) * (1 << bit)
            big = pl.ds(pl.multiple_of(a * 64, 64), 64)
            small = pl.ds(pl.multiple_of(a * 16, 16), 16)
            up[net, big, :] = one[spot, rel, 0:64, :].astype(F32)
            down[net, big, :] = one[spot, rel, 64:128, :].astype(F32)
            out[net, small, :] = one[spot, rel, 128:144, :].astype(F32)
            q[net, big, :] = two[spot, rel, :, 0:128].astype(F32)
            k[net, big, :] = two[spot, rel, :, 128:256].astype(F32)
            v[net, big, :] = two[spot, rel, :, 256:384].astype(F32)


def swap(value, axis, size, bit):
    return lax.ppermute(value, axis, [(n, n ^ bit) for n in range(size)])


def sum_rows(keep, send, seq):
    buf = keep + swap(send, "tp", 4, 1)
    size = PIECES
    for bit in ORDER:
        size //= 2
        buf = buf[:size] + swap(buf[size:], "seq", seq, 1 << bit)
    far = PIECES
    while far < seq:
        buf = buf + swap(buf, "seq", seq, far)
        far *= 2
    other = swap(buf[:, 1], "tp", 4, 2)
    buf = jnp.stack([buf[:, 0], other], axis=1)
    for bit in reversed(ORDER):
        buf = jnp.concatenate([buf, swap(buf, "seq", seq, 1 << bit)], axis=0)
    return buf


def body(layer_in, cotangent, clip_of_frame, w_query, w_key, w_value, w_out, w_up, w_down, norm1_gain, norm1_bias, norm2_gain, norm2_bias):
    seq = lax.axis_size("seq")
    frames = seq // GROUP
    i = lax.axis_index("seq")
    j = lax.axis_index("tp")
    net, core = j // 2, j % 2
    spot, frame = i % GROUP, i // GROUP
    segment, width = layer_in.shape[1], layer_in.shape[3]
    rows = segment * GROUP
    whole = jnp.where(clip_of_frame[0, frames - 1] == 0, 0, 1)
    stream = whole ^ core
    sc = jnp.stack([spot ^ j, net, place(i % PIECES)]).astype(jnp.int32)

    def mine(array):
        return lax.dynamic_slice(array, (net, 0, stream, 0), (1, segment, 1, width)).reshape(segment, width)

    x = mine(layer_in)
    cot = mine(cotangent)
    clips = lax.dynamic_index_in_dim(clip_of_frame, stream, 0, keepdims=False)
    marks = [lax.dynamic_index_in_dim(clips, frame ^ r, 0, keepdims=False) for r in range(frames)]
    act = jnp.stack([(mark == marks[0]).astype(jnp.int32) for mark in marks])

    def both(parts, axis):
        packed = jnp.concatenate(parts, axis=axis)
        own = lax.dynamic_index_in_dim(packed, net, 0, keepdims=False)
        other = lax.dynamic_index_in_dim(packed, 1 - net, 0, keepdims=False)
        got = swap(other, "tp", 4, 2)
        return own, got, swap(jnp.stack([own, got]), "tp", 4, 1)

    xs = [x] + [swap(x, "seq", seq, k) for k in range(1, GROUP)]
    w_heads = both([w_query, w_key, w_value], 2)
    w_rest = both([w_up, w_down, w_out], 1)

    (qkv,) = call(project_kernel, [((rows, 384), BF)], sc, [*xs, *w_heads, norm1_gain, norm1_bias],
                  scratch=[pltpu.VMEM((width, 384), BF)], flops=2 * rows * width * 384)

    def cross(value, r):
        if frames == 2:
            pairs = [(n * 4 + t, (n ^ GROUP) * 4 + t) for n in range(seq) for t in (0, 2)]
            return lax.ppermute(value, ("seq", "tp"), pairs)
        return swap(value, "seq", seq, GROUP * r)

    kvx = jnp.stack([cross(qkv[:, 128:384], r) for r in range(1, frames)])
    qb = 256
    o, ot, lse = call(
        lambda *refs: attend_kernel(frames, qb, *refs),
        [((rows, 128), BF), ((128, rows), F32), ((2, rows), F32)], act, [qkv, kvx],
        scratch=[pltpu.VMEM((2, rows, 128), BF), pltpu.VMEM((128, rows), BF), pltpu.VMEM((2, rows), F32),
                 pltpu.VMEM((2, rows), F32), pltpu.VMEM((128, rows), F32)], flops=8 * rows * rows * 128)
    o4 = o.reshape(GROUP, segment, 128)
    os = [o4[0]] + [swap(o4[k], "seq", seq, k) for k in range(1, GROUP)]
    do4, lout, h, du, b, dz, dy, gains2 = call(
        middle_kernel,
        [((GROUP, segment, 128), BF), ((segment, width), BF), ((segment, 2048), BF), ((segment, 2048), BF),
         ((segment, width), BF), ((segment, width), BF), ((segment, width), F32), ((2, width), F32)],
        sc, [x, cot, *os, *w_rest, norm2_gain, norm2_bias],
        scratch=[pltpu.VMEM((4, 128, width), BF)], flops=2 * segment * 512 * (2048 * 4 + 1024))
    dos = [do4[0]] + [swap(do4[k], "seq", seq, k) for k in range(1, GROUP)]
    do = jnp.concatenate(dos, axis=0)

    def grads(shards):
        (out,) = call(
            lambda *refs: middle_grads_kernel(shards, *refs), [((PIECES, 2, RUP + RDOWN + ROUT, 512), BF)],
            sc, [h, du, b, dz, cot, *os], scratch=[pltpu.VMEM((4, segment, 128), BF)], flops=4 * segment * 512 * 1152)
        return out

    send1 = grads((1, 3))
    keep1 = grads((0, 2))
    one = sum_rows(keep1, send1, seq)

    dq, dkv_own, dkv_x = call(
        lambda *refs: attend_back_kernel(frames, qb, *refs),
        [((rows, 128), BF), ((rows, 256), F32), ((frames - 1, rows, 256), BF)], act, [qkv, kvx, do, ot, lse],
        scratch=[pltpu.VMEM((2, rows, 128), BF), pltpu.VMEM((2, rows, 128), BF), pltpu.VMEM((128, rows), BF),
                 pltpu.VMEM((2, rows), F32), pltpu.VMEM((128, rows), F32), pltpu.VMEM((rows, 128), F32),
                 pltpu.VMEM((rows, 128), F32)], flops=20 * rows * rows * 128)
    total = dkv_own
    for r in range(1, frames):
        total = total + cross(dkv_x[r - 1], r).astype(F32)
    dqkv = jnp.concatenate([dq, total.astype(BF)], axis=1).reshape(GROUP, segment, 384)
    ds = [dqkv[0]] + [swap(dqkv[k], "seq", seq, k) for k in range(1, GROUP)]
    gin, gains1, keep2, send2 = call(
        input_kernel,
        [((segment, width), BF), ((2, width), F32), ((PIECES, 2, 64, 384), BF), ((PIECES, 2, 64, 384), BF)],
        sc, [x, dy, *ds, *w_heads, norm1_gain, norm1_bias],
        scratch=[pltpu.VMEM((4, width, 384), BF), pltpu.VMEM((4, segment, 384), BF)], flops=4 * segment * 512 * 1536)
    two = sum_rows(keep2, send2, seq)

    def spread(own):
        across = swap(own, "tp", 4, 2)
        pair = jnp.stack([own, across])
        other = swap(pair, "tp", 4, 1)
        nets = jnp.stack([pair, other], axis=2)
        nets = jnp.where(stream == 0, nets, nets[:, :, ::-1])
        return jnp.where(net == 0, nets, nets[::-1])

    layer_out = spread(lout)
    input_grad = spread(gin)

    small = jnp.concatenate([gains1, gains2], axis=0)
    small = jnp.where(jnp.arange(2)[:, None, None] == net, small[None], 0.0)
    for bit in (1, 2):
        small = small + swap(small, "tp", 4, bit)
    bit = 1
    while bit < seq:
        small = small + swap(small, "seq", seq, bit)
        bit *= 2

    up, down, out, gq, gk, gv = call(
        unpack_kernel,
        [((2, 512, 512), F32), ((2, 512, 512), F32), ((2, 128, 512), F32)] + [((2, 512, 128), F32)] * 3,
        sc, [one, two], flops=1000)
    return (layer_out, input_grad, gq, gk, gv, out, up, down, small[:, 0], small[:, 1], small[:, 2], small[:, 3])


def solution(mesh):
    tokens = P(None, "seq", None, None)
    columns = P(None, None, "tp")
    rows = P(None, "tp", None)
    return jax.shard_map(
        body,
        mesh=mesh,
        in_specs=(tokens, tokens, P(), columns, columns, columns, rows, columns, rows, P(), P(), P(), P()),
        out_specs=(tokens, tokens, columns, columns, columns, rows, columns, rows, P(), P(), P(), P()),
        check_vma=False,
    )
```

```python
import math

import jax
import jax.numpy as jnp
from jax import lax
from jax.experimental import pallas as pl
from jax.experimental.pallas import tpu as pltpu
from jax.sharding import PartitionSpec as P

HEAD_DIM = 64
EPS = 1e-05
BF = jnp.bfloat16
F32 = jnp.float32
VMEM_LIMIT = 50 * 1024 * 1024
OPT = {}


def tied(name, value, *deps, default=1):
    return tie(value, *deps) if OPT.get(name, default) else value


GROUP = 4
RUP, RDOWN, ROUT = 128, 128, 32
ROWS = RUP + RDOWN + ROUT
DU_AT, H_AT, B_AT, DZ_AT, O_AT, ALL = 0, 1024, 2048, 2560, 3072, 3328
RGAIN = 16
C_GELU = math.sqrt(2.0 / math.pi)


def dot(a, b, ca=1, cb=0):
    return lax.dot_general(a, b, (((ca,), (cb,)), ((), ())), preferred_element_type=F32)


def norm_parts(v):
    center = v - jnp.mean(v, axis=-1, keepdims=True)
    inv = lax.rsqrt(jnp.mean(center * center, axis=-1, keepdims=True) + EPS)
    return center * inv, inv


def norm_back(dout, hat, inv, gain):
    e = dout * gain
    mean_e = jnp.mean(e, axis=-1, keepdims=True)
    mean_eh = jnp.mean(e * hat, axis=-1, keepdims=True)
    return (e - mean_e - hat * mean_eh) * inv


def vspec():
    return pl.BlockSpec(memory_space=pltpu.VMEM)


def sspec():
    return pl.BlockSpec(memory_space=pltpu.SMEM)


def call(kernel, outs, scalars, args, scratch=(), us=1.0, name=None, after=()):
    us = OPT.get('us_' + name, us) if name else us
    count = len(args) + 1

    def run(*refs):
        kernel(*refs[:count], *refs[count + len(after):])

    return pl.pallas_call(
        run,
        out_shape=[jax.ShapeDtypeStruct(s, d) for s, d in outs],
        in_specs=[sspec()] + [vspec()] * len(args) + [pl.BlockSpec(memory_space=pl.ANY)] * len(after),
        out_specs=[vspec()] * len(outs),
        scratch_shapes=list(scratch),
        compiler_params=pltpu.CompilerParams(vmem_limit_bytes=VMEM_LIMIT),
        cost_estimate=pl.CostEstimate(flops=int(us * 1.1e9), bytes_accessed=0, transcendentals=0),
    )(scalars, *args, *after)


def pick_shard(sc, wo, wy, wc, w_s):
    for e, ref in enumerate((wo, wc, wy, wc)):
        @pl.when(sc[0] == e)
        def _(ref=ref):
            w_s[...] = ref[...]


def project_kernel(sc, x0, x1, x2, x3, wo, wy, wc, gain, bias, qkv, a_out, w_s):
    pick_shard(sc, wo, wy, wc, w_s)
    g = gain[pl.ds(sc[1], 1), :]
    b = bias[pl.ds(sc[1], 1), :]
    for k, ref in enumerate((x0, x1, x2, x3)):
        hat, _ = norm_parts(ref[...].astype(F32))
        a = (hat * g + b).astype(BF)
        out = dot(a, w_s[...])
        rows = pl.ds(k * ref.shape[0], ref.shape[0])
        a_out[rows, :] = a
        qkv[rows, 0:128] = (out[:, 0:128].astype(BF).astype(F32) * (1.0 / math.sqrt(HEAD_DIM))).astype(BF)
        qkv[rows, 128:384] = out[:, 128:384].astype(BF)


def attend_block(k, vt, qm, m_s, l_s, acc, qb, first):
    n = qm.shape[1]
    for h in range(2):
        rows = slice(h * HEAD_DIM, (h + 1) * HEAD_DIM)

        def block(b, _, h=h, rows=rows):
            cols = pl.ds(pl.multiple_of(b * qb, qb), qb)
            st = dot(k, qm[h, cols, :], 1, 1)
            m = jnp.max(st, axis=0, keepdims=True)
            if not first:
                old = m_s[h:h + 1, cols]
                m = jnp.maximum(old, m)
            pt = jnp.exp(st - m)
            total = jnp.sum(pt, axis=0, keepdims=True)
            new = dot(vt[rows, :], pt.astype(BF))
            if not first:
                fix = jnp.exp(old - m)
                total = total + l_s[h:h + 1, cols] * fix
                new = new + acc[rows, cols] * fix
            m_s[h:h + 1, cols] = m
            l_s[h:h + 1, cols] = total
            acc[rows, cols] = new
            return 0

        lax.fori_loop(0, n // qb, block, 0)


def split_heads(value, dst):
    lane = lax.broadcasted_iota(jnp.int32, value.shape, 1)
    zero = jnp.zeros_like(value)
    dst[0] = jnp.where(lane < HEAD_DIM, value, zero)
    dst[1] = jnp.where(lane < HEAD_DIM, zero, value)


def attend_own_kernel(qb, act, qkv, qm, m_s, l_s, acc, vt):
    split_heads(qkv[:, 0:128], qm)
    vt[...] = qkv[:, 256:384].T
    attend_block(qkv[:, 128:256], vt, qm, m_s, l_s, acc, qb, True)


def attend_cross_kernel(qb, act, qm, m_in, l_in, acc_in, *refs):
    kvx = refs[:-7]
    o_out, ot_out, lse_out, m_s, l_s, acc, vt = refs[-7:]
    m_s[...] = m_in[...]
    l_s[...] = l_in[...]
    acc[...] = acc_in[...]
    for r, kv in enumerate(kvx):
        @pl.when(act[r + 1] != 0)
        def _(kv=kv):
            vt[...] = kv[:, 128:256].T
            attend_block(kv[:, 0:128], vt, qm, m_s, l_s, acc, qb, False)
    for h in range(2):
        rows = slice(h * HEAD_DIM, (h + 1) * HEAD_DIM)
        ot_out[rows, :] = acc[rows, :] / l_s[h:h + 1, :]
        lse_out[h:h + 1, :] = m_s[h:h + 1, :] + jnp.log(l_s[h:h + 1, :])
    o_out[...] = ot_out[...].T.astype(BF)


def back_block(k, v, qm, dom, lse, delta, kt, dk_s, dv_s, dqt, qb):
    kt[...] = k.T
    dk_s[...] = jnp.zeros_like(dk_s)
    dv_s[...] = jnp.zeros_like(dv_s)
    n = qm.shape[1]
    for h in range(2):
        rows = slice(h * HEAD_DIM, (h + 1) * HEAD_DIM)

        def block(b, _, h=h, rows=rows):
            cols = pl.ds(pl.multiple_of(b * qb, qb), qb)
            qh = qm[h, cols, :]
            dh = dom[h, cols, :]
            pt = jnp.exp(dot(k, qh, 1, 1) - lse[h:h + 1, cols])
            dv_s[...] += dot(pt.astype(BF), dh)
            dst = (pt * (dot(v, dh, 1, 1) - delta[h:h + 1, cols])).astype(BF)
            dk_s[...] += dot(dst, qh)
            dqt[rows, cols] += dot(kt[rows, :], dst)
            return 0

        lax.fori_loop(0, n // qb, block, 0)


def back_cross_kernel(qb, frames, act, d0, d1, d2, d3, qm, ot, lse, *refs):
    kvx, refs = refs[:frames - 1], refs[frames - 1:]
    dkv_x, (dom, delta, dqt, kt, dk_s, dv_s) = refs[:frames - 1], refs[frames - 1:]
    seg = d0.shape[0]
    for k, ref in enumerate((d0, d1, d2, d3)):
        cols = slice(k * seg, (k + 1) * seg)
        d = ref[...]
        split_heads(d, dom.at[:, cols, :])
        dt = d.astype(F32).T * ot[:, cols]
        for h in range(2):
            delta[h:h + 1, cols] = jnp.sum(dt[h * HEAD_DIM:(h + 1) * HEAD_DIM, :], axis=0, keepdims=True)
    dqt[...] = jnp.zeros_like(dqt)
    for r in range(frames - 1):
        @pl.when(act[r + 1] != 0)
        def _(r=r):
            back_block(kvx[r][:, 0:128], kvx[r][:, 128:256], qm, dom, lse, delta, kt, dk_s, dv_s, dqt, qb)
            dkv_x[r][:, 0:128] = dk_s[...].astype(BF)
            dkv_x[r][:, 128:256] = dv_s[...].astype(BF)

        @pl.when(act[r + 1] == 0)
        def _(r=r):
            dkv_x[r][...] = jnp.zeros_like(dkv_x[r])


def back_own_kernel(qb, act, qkv, qm, dom, lse, delta, dqt_in, dq_out, dkv_own, dqt, kt, dk_s, dv_s):
    dqt[...] = dqt_in[...]
    back_block(qkv[:, 128:256], qkv[:, 256:384], qm, dom, lse, delta, kt, dk_s, dv_s, dqt, qb)
    dkv_own[:, 0:128] = dk_s[...]
    dkv_own[:, 128:256] = dv_s[...]
    dq_out[...] = (dqt[...].T * (1.0 / math.sqrt(HEAD_DIM))).astype(BF)


def gelu_parts(u):
    t = jnp.tanh(C_GELU * (u + 0.044715 * (u * u * u)))
    value = 0.5 * u * (1.0 + t)
    slope = 0.5 * (1.0 + t) + 0.5 * u * (1.0 - t * t) * (C_GELU * (1.0 + 3 * 0.044715 * (u * u)))
    return value, slope


def middle_kernel(sc, x, g, o0, o1, o2, o3, w0, w1, w2, w3, gain, bias, do_out, lout, keep, send, dy_out, gains, wo_s, o_s):
    mats = (w0, w1, w2, w3)
    for e in range(4):
        wo_s[e] = mats[e][1024:1152, :]
    gain_row = gain[pl.ds(sc[1], 1), :]
    mid = x[...].astype(F32)
    for k, ref in enumerate((o0, o1, o2, o3)):
        o_s[k] = ref[...]
        mid = mid + dot(ref[...], wo_s[sc[0] ^ k])
    hat, inv = norm_parts(mid)
    b = (hat * gain_row + bias[pl.ds(sc[1], 1), :]).astype(BF)
    cot = g[...]
    dy_out[...] = mid
    db = jnp.zeros_like(mid)
    for e in range(4):
        up = mats[e][0:512, :]
        down = mats[e][512:1024, :]
        value, slope = gelu_parts(dot(b, up))
        h = value.astype(BF)
        pack, spot = (keep, send)[e % 2], 512 * (e // 2)
        pack[:, H_AT + spot:H_AT + spot + 512] = h
        dy_out[...] += dot(h, down)
        du = (dot(cot, down, 1, 1) * slope).astype(BF)
        pack[:, DU_AT + spot:DU_AT + spot + 512] = du
        db = db + dot(du, up, 1, 1)
    lout[...] = dy_out[...].astype(BF)
    gains[0:1, :] = jnp.sum(db * hat, axis=0, keepdims=True)
    gains[1:2, :] = jnp.sum(db, axis=0, keepdims=True)
    dy = cot.astype(F32) + norm_back(db, hat, inv, gain_row)
    dy_out[...] = dy
    dz = dy.astype(BF)
    for e in range(4):
        pack, spot = (keep, send)[e % 2], 128 * (e // 2)
        pack[:, O_AT + spot:O_AT + spot + 128] = o_s[sc[0] ^ e]
    for pack in (keep, send):
        pack[:, B_AT:B_AT + 512] = b
        pack[:, DZ_AT:DZ_AT + 512] = dz
    for k in range(4):
        do_out[k] = dot(dz, wo_s[sc[0] ^ k], 1, 1).astype(BF)


def store_pieces(dst, e, row, value, rows, sc):
    for a in range(GROUP):
        dst[a ^ sc[2], e, row:row + rows, :] = value[a * rows:(a + 1) * rows, :]


def grads_kernel(sc, mine, other, g_mine, g_other, out, both, g):
    n = mine.shape[0]
    both[0:n, :] = mine[...]
    both[n:2 * n, :] = other[...]
    g[0:n, :] = g_mine[...]
    g[n:2 * n, :] = g_other[...]
    for e in range(2):
        du = both[:, DU_AT + 512 * e:DU_AT + 512 * e + 512]
        h = both[:, H_AT + 512 * e:H_AT + 512 * e + 512]
        o = both[:, O_AT + 128 * e:O_AT + 128 * e + 128]
        store_pieces(out, e, 0, dot(both[:, B_AT:B_AT + 512], du, 0, 0).astype(BF), RUP, sc)
        store_pieces(out, e, RUP, dot(h, g[...], 0, 0).astype(BF), RDOWN, sc)
        store_pieces(out, e, RUP + RDOWN, dot(o, both[:, DZ_AT:DZ_AT + 512], 0, 0).astype(BF), ROUT, sc)


def grads_heads_kernel(sc, a, dqkv, keep, send):
    grad = dot(a[...], dqkv[...], 0, 0).astype(BF)
    size = grad.shape[0] // 2
    for n in range(2):
        @pl.when(sc[3] == n)
        def _(n=n):
            keep[...] = grad[n * size:(n + 1) * size, :]
            send[...] = grad[(1 - n) * size:(2 - n) * size, :]


def input_kernel(sc, x, dy, d0, d1, d2, d3, w0, w1, w2, w3, gain, bias, gains2, lout, pack, gains, w_s):
    mats = (w0, w1, w2, w3)
    for e in range(4):
        w_s[e] = mats[e][...]
    gain_row = gain[pl.ds(sc[1], 1), :]
    hat, inv = norm_parts(x[...].astype(F32))
    da = jnp.zeros_like(hat)
    for k, ref in enumerate((d0, d1, d2, d3)):
        da = da + dot(ref[...], w_s[sc[0] ^ k], 1, 1)
    n = x.shape[0]
    pack[0:n, :] = (dy[...] + norm_back(da, hat, inv, gain_row)).astype(BF)
    pack[n:2 * n, :] = lout[...]
    gains[...] = jnp.zeros_like(gains)
    gains[0:1, :] = jnp.sum(da * hat, axis=0, keepdims=True)
    gains[1:2, :] = jnp.sum(da, axis=0, keepdims=True)
    gains[2:4, :] = gains2[...]


def unpack_kernel(sc, p0, p1, p2, p3, up, down, out, gains):
    total = jnp.zeros((RGAIN, 512), F32)
    for k, src in enumerate((p0, p1, p2, p3)):
        a = k ^ sc[2]
        for rel in range(2):
            net, row = sc[1] ^ rel, rel * ROWS
            up[net, pl.ds(pl.multiple_of(a * RUP, RUP), RUP), :] = src[row:row + RUP, :].astype(F32)
            down[net, pl.ds(pl.multiple_of(a * RDOWN, RDOWN), RDOWN), :] = src[row + RUP:row + RUP + RDOWN, :].astype(F32)
            out[net, pl.ds(pl.multiple_of(a * ROUT, ROUT), ROUT), :] = src[row + RUP + RDOWN:row + ROWS, :].astype(F32)
        total = total + src[2 * ROWS:2 * ROWS + RGAIN, :].astype(F32)
    gains[sc[1]] = total[0:8, :]
    gains[sc[1] ^ 1] = total[8:16, :]


def unpack_heads_kernel(sc, mine, other, q, k, v):
    size = mine.shape[1]
    for rel in range(2):
        net = sc[1] ^ rel
        for core, src in enumerate((mine, other)):
            rows = pl.ds(pl.multiple_of((core ^ sc[3]) * size, size), size)
            q[net, rows, :] = src[rel, :, 0:128].astype(F32)
            k[net, rows, :] = src[rel, :, 128:256].astype(F32)
            v[net, rows, :] = src[rel, :, 256:384].astype(F32)


def swap(value, axis, size, bit):
    return lax.ppermute(value, axis, [(n, n ^ bit) for n in range(size)])


def tie(value, *deps):
    return lax.optimization_barrier((value, deps))[0]


def body(layer_in, cotangent, clip_of_frame, w_query, w_key, w_value, w_out, w_up, w_down, norm1_gain, norm1_bias, norm2_gain, norm2_bias):
    seq = lax.axis_size("seq")
    frames = seq // GROUP
    i = lax.axis_index("seq")
    j = lax.axis_index("tp")
    net, core = j // 2, j % 2
    spot, frame = i % GROUP, i // GROUP
    segment, width = layer_in.shape[1], layer_in.shape[3]
    rows = segment * GROUP
    whole = jnp.where(clip_of_frame[0, frames - 1] == 0, 0, 1)
    stream = whole ^ core

    def mine(array, stream):
        return lax.dynamic_slice(array, (net, 0, stream, 0), (1, segment, 1, width)).reshape(segment, width)

    x = mine(layer_in, stream)
    cot = mine(cotangent, stream)
    cot_other = mine(cotangent, 1 - stream)
    clips = lax.dynamic_index_in_dim(clip_of_frame, stream, 0, keepdims=False)
    marks = [lax.dynamic_index_in_dim(clips, frame ^ r, 0, keepdims=False) for r in range(frames)]
    act = jnp.stack([(mark == marks[0]).astype(jnp.int32) for mark in marks])
    sc = jnp.concatenate([jnp.stack([spot ^ j, net, spot, core]).astype(jnp.int32), act[1:]])

    def nets_of(parts, axis):
        packed = jnp.concatenate(parts, axis=axis)
        own = lax.dynamic_index_in_dim(packed, net, 0, keepdims=False)
        other = lax.dynamic_index_in_dim(packed, 1 - net, 0, keepdims=False)
        return own, other

    def across(value):
        return swap(value, "tp", 4, 2)

    def beside(value):
        return swap(value, "tp", 4, 1)

    def to_group(chunks, only=None):
        out = [chunks[0]]
        for k in range(1, GROUP):
            if only is None:
                out.append(swap(chunks[k], "seq", seq, k))
            else:
                pairs = [(n * 4 + t, (n ^ k) * 4 + t) for n in range(seq) for t in only]
                out.append(lax.ppermute(chunks[k], ("seq", "tp"), pairs))
        return out

    def chunks_of(array):
        return [array[k * segment:(k + 1) * segment] for k in range(GROUP)]

    paired = (0, 2) if frames == 2 else (0, 1, 2, 3)

    def cross(value, r):
        pairs = [(n * 4 + t, (n ^ (GROUP * r)) * 4 + t) for n in range(seq) for t in paired]
        return lax.ppermute(value, ("seq", "tp"), pairs)

    xs = to_group([x] * GROUP)
    head_own, head_other = nets_of([w_query, w_key, w_value], 2)
    spots = [(n * 4, n % GROUP) for n in range(seq)]
    unit_y = lax.ppermute(tie(head_other, x), ("seq", "tp"), [(n + p, n + (p ^ 2)) for n, p in spots])
    unit = jnp.where(spot == j, head_own, unit_y)
    unit_c = lax.ppermute(unit, ("seq", "tp"), [(n + q, n + (q ^ 1)) for n, p in spots for q in (p, p ^ 2)])
    rest_own, rest_other = nets_of([w_up, w_down, w_out], 1)
    rest_y = across(tie(rest_other, unit_y))

    qkv, a = call(project_kernel, [((rows, 384), BF), ((rows, width), BF)], sc, [*xs, head_own, unit_y, unit_c, norm1_gain, norm1_bias],
                  scratch=[pltpu.VMEM((width, 384), BF)], us=2, name="k1")
    qb = 256
    kvx = [cross(qkv[:, 128:384], r) for r in range(1, frames)]
    qm, m_own, l_own, acc_own = call(
        lambda *refs: attend_own_kernel(qb, *refs),
        [((2, rows, 128), BF), ((2, rows), F32), ((2, rows), F32), ((128, rows), F32)], act, [qkv],
        scratch=[pltpu.VMEM((128, rows), BF)], us=7, name="own")
    o, ot, lse = call(
        lambda *refs: attend_cross_kernel(qb, *refs),
        [((rows, 128), BF), ((128, rows), F32), ((2, rows), F32)], act, [qm, m_own, l_own, acc_own, *kvx],
        scratch=[pltpu.VMEM((2, rows), F32), pltpu.VMEM((2, rows), F32), pltpu.VMEM((128, rows), F32),
                 pltpu.VMEM((128, rows), BF)], us=7, name="cross")

    os = to_group(chunks_of(o))
    head_y = across(tied('head_y', head_other, rest_y))
    rest = [rest_own, beside(tied('rest_c', rest_own, m_own)), rest_y, beside(tied('rest_yc', rest_y, o))]
    do4, lout, keep, send, dy, gains2 = call(
        middle_kernel,
        [((GROUP, segment, 128), BF), ((segment, width), BF), ((segment, ALL), BF), ((segment, ALL), BF),
         ((segment, width), F32), ((2, width), F32)],
        sc, [x, cot, *os, *rest, norm2_gain, norm2_bias],
        scratch=[pltpu.VMEM((4, 128, width), BF), pltpu.VMEM((4, segment, 128), BF)], us=8, name="mid")
    dos = to_group([do4[k] for k in range(GROUP)])

    (chip,) = call(
        grads_kernel, [((GROUP, 2, ROWS, 512), BF)], sc, [keep, beside(send), cot, cot_other],
        scratch=[pltpu.VMEM((2 * segment, ALL), BF), pltpu.VMEM((2 * segment, width), BF)], us=4, name="grads")

    def add(*terms):
        total = terms[0].astype(F32)
        for term in terms[1:]:
            total = total + term.astype(F32)
        return total.astype(BF)

    def over_frames(value, *deps):
        bit = GROUP
        while bit < seq:
            value = add(value, tie(swap(value, "seq", seq, bit), *deps))
            bit *= 2
        return value

    def add_group(parts, *deps):
        return add(parts[0], *[tie(part, *deps) for part in parts[1:]])

    head_c = beside(tie(head_own, o))
    head_yc = beside(tie(head_y, chip))
    head = [head_own, head_c, head_y, head_yc]
    group = to_group([chip[k] for k in range(GROUP)])
    back = call(
        lambda *refs: back_cross_kernel(qb, frames, *refs),
        [((rows, 256), BF)] * (frames - 1) + [((2, rows, 128), BF), ((2, rows), F32), ((128, rows), F32)],
        tie(act, chip, head_c, head_y), [*dos, qm, ot, lse, *kvx],
        scratch=[pltpu.VMEM((128, rows), BF), pltpu.VMEM((rows, 128), F32), pltpu.VMEM((rows, 128), F32)], us=8, name="bx")
    dkv_x, (dom, delta, dqt) = back[:frames - 1], back[frames - 1:]
    dkv_far = [cross(dkv_x[r - 1], r) for r in range(1, frames)]
    dq, dkv_own = call(
        lambda *refs: back_own_kernel(qb, *refs),
        [((rows, 128), BF), ((rows, 256), F32)], tie(act, group[1], group[2], dqt, head_yc), [qkv, qm, dom, lse, delta, dqt],
        scratch=[pltpu.VMEM((128, rows), F32), pltpu.VMEM((128, rows), BF), pltpu.VMEM((rows, 128), F32),
                 pltpu.VMEM((rows, 128), F32)], us=8, name="bo")
    total = dkv_own
    for far in dkv_far:
        total = total + far.astype(F32)
    dqkv = jnp.concatenate([dq, total.astype(BF)], axis=1)
    ds = to_group(chunks_of(dqkv))

    keep_c, send_c = call(grads_heads_kernel, [((width // 2, 384), BF)] * 2, sc, [a, dqkv], us=2, name="kc")
    sum_c = add(keep_c, beside(send_c))
    mine = add(group[0], *[tied("mine", part, sum_c) for part in group[1:]])
    net_0 = mine[0]
    bit = GROUP
    got_0 = swap(net_0, "seq", seq, GROUP)
    got_c = swap(tied("c_mine", sum_c, mine), "seq", seq, GROUP)

    pack, gains = call(
        input_kernel, [((2 * segment, width), BF), ((RGAIN, width), F32)],
        tied("k5_m", sc, mine), [x, dy, *ds, *head, norm1_gain, norm1_bias, gains2, lout],
        scratch=[pltpu.VMEM((4, width, 384), BF)], us=2, name="k5")
    gains = tied('g_0', gains, got_0)
    gains = add(gains, beside(gains))
    cross_y = across(jnp.concatenate([mine[1], gains]))
    gains = jnp.where(jnp.arange(RGAIN)[:, None] < 8, gains, jnp.roll(cross_y[ROWS:], 8, axis=0))
    net_1 = jnp.concatenate([cross_y[:ROWS], gains])
    pack = tied('pack_y', pack, cross_y)
    pack_y = across(pack)
    sum_c = add(sum_c, tied("c2_y", got_c, cross_y))
    net_0 = add(net_0, tied("n0_y", got_0, cross_y))
    got_1 = swap(net_1, "seq", seq, GROUP)
    all_c = jnp.stack(to_group([tied('c_n1', sum_c, net_1)] * GROUP))
    all_c = tied('c_g1', all_c, got_1)
    net_1 = add(net_1, tied("n1_c", got_1, all_c, default=0))
    bit = 2 * GROUP
    while bit < seq:
        sum_c, net_0, net_1 = [add(value, swap(value, "seq", seq, bit)) for value in (sum_c, net_0, net_1)]
        bit *= 2
    all_g = to_group([tied("ag_py", jnp.concatenate([net_0, net_1]), pack_y, default=0)] * GROUP)

    def shard(number):
        return lax.dynamic_index_in_dim(all_c, spot ^ number, 0, keepdims=False)

    far_c = across(jnp.stack([shard(j ^ 2), shard(j ^ 3)]))
    mine_c = jnp.stack([shard(j), far_c[0]])
    other_c = beside(jnp.stack([shard(j ^ 1), far_c[1]]))

    def spread(own, far, own_c, far_c):
        out = []
        for n in range(2):
            near = net == n
            mine_n = jnp.where(near, own, far)
            other_n = jnp.where(near, own_c, far_c)
            out.append(jnp.stack([jnp.where(stream == s, mine_n, other_n) for s in range(2)], axis=1))
        return jnp.stack(out)

    pack = tied('pack_y', pack, cross_y)
    pack_y = across(pack)
    packs = [pack, pack_y, beside(tied('pc', pack, pack_y)), beside(pack_y)]
    input_grad = spread(*[part[:segment] for part in packs])
    layer_out = spread(*[part[segment:] for part in packs])
    gq, gk, gv = call(unpack_heads_kernel, [((2, 512, 128), F32)] * 3, sc, [mine_c, other_c], us=1, name="uc")
    up, down, out, gains = call(
        unpack_kernel, [((2, 512, 512), F32), ((2, 512, 512), F32), ((2, 128, 512), F32), ((2, 8, width), F32)],
        tie(sc, gq, layer_out, input_grad), all_g, us=3, name="up")
    return (layer_out, input_grad, gq, gk, gv, out, up, down, gains[:, 0], gains[:, 1], gains[:, 2], gains[:, 3])


def solution(mesh):
    tokens = P(None, "seq", None, None)
    columns = P(None, None, "tp")
    rows = P(None, "tp", None)
    return jax.shard_map(
        body,
        mesh=mesh,
        in_specs=(tokens, tokens, P(), columns, columns, columns, rows, columns, rows, P(), P(), P(), P()),
        out_specs=(tokens, tokens, columns, columns, columns, rows, columns, rows, P(), P(), P(), P()),
        check_vma=False,
    )
```

```python
import math

import jax
import jax.numpy as jnp
from jax import lax
from jax.experimental import pallas as pl
from jax.experimental.pallas import tpu as pltpu
from jax.sharding import PartitionSpec as P

HEAD_DIM = 64
EPS = 1e-05
BF = jnp.bfloat16
F32 = jnp.float32
VMEM_LIMIT = 50 * 1024 * 1024
OPT = {"scale": 10}


def tied(name, value, *deps, default=1):
    return tie(value, *deps) if OPT.get(name, default) else value


GROUP = 4
RUP, RDOWN, ROUT = 128, 128, 32
ROWS = RUP + RDOWN + ROUT
DU_AT, H_AT, B_AT, DZ_AT, O_AT, ALL = 0, 1024, 2048, 2560, 3072, 3328
RGAIN = 16
C_GELU = math.sqrt(2.0 / math.pi)


def dot(a, b, ca=1, cb=0):
    return lax.dot_general(a, b, (((ca,), (cb,)), ((), ())), preferred_element_type=F32)


def norm_parts(v):
    center = v - jnp.mean(v, axis=-1, keepdims=True)
    inv = lax.rsqrt(jnp.mean(center * center, axis=-1, keepdims=True) + EPS)
    return center * inv, inv


def norm_back(dout, hat, inv, gain):
    e = dout * gain
    mean_e = jnp.mean(e, axis=-1, keepdims=True)
    mean_eh = jnp.mean(e * hat, axis=-1, keepdims=True)
    return (e - mean_e - hat * mean_eh) * inv


def vspec():
    return pl.BlockSpec(memory_space=pltpu.VMEM)


def sspec():
    return pl.BlockSpec(memory_space=pltpu.SMEM)


def call(kernel, outs, scalars, args, scratch=(), us=1.0, name=None, after=()):
    us = OPT.get('us_' + name, us) if name else us
    count = len(args) + 1

    def run(*refs):
        kernel(*refs[:count], *refs[count + len(after):])

    return pl.pallas_call(
        run,
        out_shape=[jax.ShapeDtypeStruct(s, d) for s, d in outs],
        in_specs=[sspec()] + [vspec()] * len(args) + [pl.BlockSpec(memory_space=pl.ANY)] * len(after),
        out_specs=[vspec()] * len(outs),
        scratch_shapes=list(scratch),
        compiler_params=pltpu.CompilerParams(vmem_limit_bytes=VMEM_LIMIT),
        cost_estimate=pl.CostEstimate(flops=int(us * 1.1e9 * OPT.get("scale", 1)), bytes_accessed=0, transcendentals=0),
    )(scalars, *args, *after)


def pick_shard(sc, wo, wy, wc, w_s):
    for e, ref in enumerate((wo, wc, wy, wc)):
        @pl.when(sc[0] == e)
        def _(ref=ref):
            w_s[...] = ref[...]


def project_kernel(sc, x0, x1, x2, x3, wo, wy, wc, gain, bias, qkv, a_out, w_s):
    pick_shard(sc, wo, wy, wc, w_s)
    g = gain[pl.ds(sc[1], 1), :]
    b = bias[pl.ds(sc[1], 1), :]
    for k, ref in enumerate((x0, x1, x2, x3)):
        hat, _ = norm_parts(ref[...].astype(F32))
        a = (hat * g + b).astype(BF)
        out = dot(a, w_s[...])
        rows = pl.ds(k * ref.shape[0], ref.shape[0])
        a_out[rows, :] = a
        qkv[rows, 0:128] = (out[:, 0:128].astype(BF).astype(F32) * (1.0 / math.sqrt(HEAD_DIM))).astype(BF)
        qkv[rows, 128:384] = out[:, 128:384].astype(BF)


def attend_block(k, vt, qm, m_s, l_s, acc, qb, first):
    n = qm.shape[1]
    for h in range(2):
        rows = slice(h * HEAD_DIM, (h + 1) * HEAD_DIM)

        def block(b, _, h=h, rows=rows):
            cols = pl.ds(pl.multiple_of(b * qb, qb), qb)
            st = dot(k, qm[h, cols, :], 1, 1)
            m = jnp.max(st, axis=0, keepdims=True)
            if not first:
                old = m_s[h:h + 1, cols]
                m = jnp.maximum(old, m)
            pt = jnp.exp(st - m)
            total = jnp.sum(pt, axis=0, keepdims=True)
            new = dot(vt[rows, :], pt.astype(BF))
            if not first:
                fix = jnp.exp(old - m)
                total = total + l_s[h:h + 1, cols] * fix
                new = new + acc[rows, cols] * fix
            m_s[h:h + 1, cols] = m
            l_s[h:h + 1, cols] = total
            acc[rows, cols] = new
            return 0

        lax.fori_loop(0, n // qb, block, 0)


def split_heads(value, dst):
    lane = lax.broadcasted_iota(jnp.int32, value.shape, 1)
    zero = jnp.zeros_like(value)
    dst[0] = jnp.where(lane < HEAD_DIM, value, zero)
    dst[1] = jnp.where(lane < HEAD_DIM, zero, value)


def attend_own_kernel(qb, act, qkv, qm, m_s, l_s, acc, vt):
    split_heads(qkv[:, 0:128], qm)
    vt[...] = qkv[:, 256:384].T
    attend_block(qkv[:, 128:256], vt, qm, m_s, l_s, acc, qb, True)


def attend_cross_kernel(qb, act, qm, m_in, l_in, acc_in, *refs):
    kvx = refs[:-7]
    o_out, ot_out, lse_out, m_s, l_s, acc, vt = refs[-7:]
    m_s[...] = m_in[...]
    l_s[...] = l_in[...]
    acc[...] = acc_in[...]
    for r, kv in enumerate(kvx):
        @pl.when(act[r + 1] != 0)
        def _(kv=kv):
            vt[...] = kv[:, 128:256].T
            attend_block(kv[:, 0:128], vt, qm, m_s, l_s, acc, qb, False)
    for h in range(2):
        rows = slice(h * HEAD_DIM, (h + 1) * HEAD_DIM)
        ot_out[rows, :] = acc[rows, :] / l_s[h:h + 1, :]
        lse_out[h:h + 1, :] = m_s[h:h + 1, :] + jnp.log(l_s[h:h + 1, :])
    o_out[...] = ot_out[...].T.astype(BF)


def back_block(k, v, qm, dom, lse, delta, kt, dk_s, dv_s, dqt, qb):
    kt[...] = k.T
    dk_s[...] = jnp.zeros_like(dk_s)
    dv_s[...] = jnp.zeros_like(dv_s)
    n = qm.shape[1]
    for h in range(2):
        rows = slice(h * HEAD_DIM, (h + 1) * HEAD_DIM)

        def block(b, _, h=h, rows=rows):
            cols = pl.ds(pl.multiple_of(b * qb, qb), qb)
            qh = qm[h, cols, :]
            dh = dom[h, cols, :]
            pt = jnp.exp(dot(k, qh, 1, 1) - lse[h:h + 1, cols])
            dv_s[...] += dot(pt.astype(BF), dh)
            dst = (pt * (dot(v, dh, 1, 1) - delta[h:h + 1, cols])).astype(BF)
            dk_s[...] += dot(dst, qh)
            dqt[rows, cols] += dot(kt[rows, :], dst)
            return 0

        lax.fori_loop(0, n // qb, block, 0)


def back_cross_kernel(qb, frames, act, d0, d1, d2, d3, qm, ot, lse, *refs):
    kvx, refs = refs[:frames - 1], refs[frames - 1:]
    dkv_x, (dom, delta, dqt, kt, dk_s, dv_s) = refs[:frames - 1], refs[frames - 1:]
    seg = d0.shape[0]
    for k, ref in enumerate((d0, d1, d2, d3)):
        cols = slice(k * seg, (k + 1) * seg)
        d = ref[...]
        split_heads(d, dom.at[:, cols, :])
        dt = d.astype(F32).T * ot[:, cols]
        for h in range(2):
            delta[h:h + 1, cols] = jnp.sum(dt[h * HEAD_DIM:(h + 1) * HEAD_DIM, :], axis=0, keepdims=True)
    dqt[...] = jnp.zeros_like(dqt)
    for r in range(frames - 1):
        @pl.when(act[r + 1] != 0)
        def _(r=r):
            back_block(kvx[r][:, 0:128], kvx[r][:, 128:256], qm, dom, lse, delta, kt, dk_s, dv_s, dqt, qb)
            dkv_x[r][:, 0:128] = dk_s[...].astype(BF)
            dkv_x[r][:, 128:256] = dv_s[...].astype(BF)

        @pl.when(act[r + 1] == 0)
        def _(r=r):
            dkv_x[r][...] = jnp.zeros_like(dkv_x[r])


def back_own_kernel(qb, act, qkv, qm, dom, lse, delta, dqt_in, dq_out, dkv_own, dqt, kt, dk_s, dv_s):
    dqt[...] = dqt_in[...]
    back_block(qkv[:, 128:256], qkv[:, 256:384], qm, dom, lse, delta, kt, dk_s, dv_s, dqt, qb)
    dkv_own[:, 0:128] = dk_s[...]
    dkv_own[:, 128:256] = dv_s[...]
    dq_out[...] = (dqt[...].T * (1.0 / math.sqrt(HEAD_DIM))).astype(BF)


def gelu_parts(u):
    t = jnp.tanh(C_GELU * (u + 0.044715 * (u * u * u)))
    value = 0.5 * u * (1.0 + t)
    slope = 0.5 * (1.0 + t) + 0.5 * u * (1.0 - t * t) * (C_GELU * (1.0 + 3 * 0.044715 * (u * u)))
    return value, slope


def middle_kernel(sc, x, g, o0, o1, o2, o3, w0, w1, w2, w3, gain, bias, do_out, lout, keep, send, dy_out, gains, wo_s, o_s):
    mats = (w0, w1, w2, w3)
    for e in range(4):
        wo_s[e] = mats[e][1024:1152, :]
    gain_row = gain[pl.ds(sc[1], 1), :]
    mid = x[...].astype(F32)
    for k, ref in enumerate((o0, o1, o2, o3)):
        o_s[k] = ref[...]
        mid = mid + dot(ref[...], wo_s[sc[0] ^ k])
    hat, inv = norm_parts(mid)
    b = (hat * gain_row + bias[pl.ds(sc[1], 1), :]).astype(BF)
    cot = g[...]
    dy_out[...] = mid
    db = jnp.zeros_like(mid)
    for e in range(4):
        up = mats[e][0:512, :]
        down = mats[e][512:1024, :]
        value, slope = gelu_parts(dot(b, up))
        h = value.astype(BF)
        pack, spot = (keep, send)[e % 2], 512 * (e // 2)
        pack[:, H_AT + spot:H_AT + spot + 512] = h
        dy_out[...] += dot(h, down)
        du = (dot(cot, down, 1, 1) * slope).astype(BF)
        pack[:, DU_AT + spot:DU_AT + spot + 512] = du
        db = db + dot(du, up, 1, 1)
    lout[...] = dy_out[...].astype(BF)
    gains[0:1, :] = jnp.sum(db * hat, axis=0, keepdims=True)
    gains[1:2, :] = jnp.sum(db, axis=0, keepdims=True)
    dy = cot.astype(F32) + norm_back(db, hat, inv, gain_row)
    dy_out[...] = dy
    dz = dy.astype(BF)
    for e in range(4):
        pack, spot = (keep, send)[e % 2], 128 * (e // 2)
        pack[:, O_AT + spot:O_AT + spot + 128] = o_s[sc[0] ^ e]
    for pack in (keep, send):
        pack[:, B_AT:B_AT + 512] = b
        pack[:, DZ_AT:DZ_AT + 512] = dz
    for k in range(4):
        do_out[k] = dot(dz, wo_s[sc[0] ^ k], 1, 1).astype(BF)


def store_pieces(dst, e, row, value, rows, sc):
    for a in range(GROUP):
        dst[a ^ sc[2], e, row:row + rows, :] = value[a * rows:(a + 1) * rows, :]


def grads_kernel(sc, mine, other, g_mine, g_other, out, both, g):
    n = mine.shape[0]
    both[0:n, :] = mine[...]
    both[n:2 * n, :] = other[...]
    g[0:n, :] = g_mine[...]
    g[n:2 * n, :] = g_other[...]
    for e in range(2):
        du = both[:, DU_AT + 512 * e:DU_AT + 512 * e + 512]
        h = both[:, H_AT + 512 * e:H_AT + 512 * e + 512]
        o = both[:, O_AT + 128 * e:O_AT + 128 * e + 128]
        store_pieces(out, e, 0, dot(both[:, B_AT:B_AT + 512], du, 0, 0).astype(BF), RUP, sc)
        store_pieces(out, e, RUP, dot(h, g[...], 0, 0).astype(BF), RDOWN, sc)
        store_pieces(out, e, RUP + RDOWN, dot(o, both[:, DZ_AT:DZ_AT + 512], 0, 0).astype(BF), ROUT, sc)


def grads_heads_kernel(sc, a, dqkv, keep, send):
    grad = dot(a[...], dqkv[...], 0, 0).astype(BF)
    size = grad.shape[0] // 2
    for n in range(2):
        @pl.when(sc[3] == n)
        def _(n=n):
            keep[...] = grad[n * size:(n + 1) * size, :]
            send[...] = grad[(1 - n) * size:(2 - n) * size, :]


def input_kernel(sc, x, dy, d0, d1, d2, d3, w0, w1, w2, w3, gain, bias, gains2, gin, gains, w_s):
    mats = (w0, w1, w2, w3)
    for e in range(4):
        w_s[e] = mats[e][...]
    gain_row = gain[pl.ds(sc[1], 1), :]
    hat, inv = norm_parts(x[...].astype(F32))
    da = jnp.zeros_like(hat)
    for k, ref in enumerate((d0, d1, d2, d3)):
        da = da + dot(ref[...], w_s[sc[0] ^ k], 1, 1)
    gin[...] = (dy[...] + norm_back(da, hat, inv, gain_row)).astype(BF)
    gains[...] = jnp.zeros_like(gains)
    gains[0:1, :] = jnp.sum(da * hat, axis=0, keepdims=True)
    gains[1:2, :] = jnp.sum(da, axis=0, keepdims=True)
    gains[2:4, :] = gains2[...]


def unpack_kernel(sc, p0, p1, p2, p3, q0, q1, q2, q3, up, down, out):
    for rel, parts in enumerate(((p0, p1, p2, p3), (q0, q1, q2, q3))):
        net = sc[1] ^ rel
        for k, src in enumerate(parts):
            a = k ^ sc[2]
            up[net, pl.ds(pl.multiple_of(a * RUP, RUP), RUP), :] = src[0:RUP, :].astype(F32)
            down[net, pl.ds(pl.multiple_of(a * RDOWN, RDOWN), RDOWN), :] = src[RUP:RUP + RDOWN, :].astype(F32)
            out[net, pl.ds(pl.multiple_of(a * ROUT, ROUT), ROUT), :] = src[RUP + RDOWN:ROWS, :].astype(F32)

def unpack_heads_kernel(sc, mine, other, q, k, v):
    size = mine.shape[1]
    for rel in range(2):
        net = sc[1] ^ rel
        for core, src in enumerate((mine, other)):
            rows = pl.ds(pl.multiple_of((core ^ sc[3]) * size, size), size)
            q[net, rows, :] = src[rel, :, 0:128].astype(F32)
            k[net, rows, :] = src[rel, :, 128:256].astype(F32)
            v[net, rows, :] = src[rel, :, 256:384].astype(F32)


def swap(value, axis, size, bit):
    return lax.ppermute(value, axis, [(n, n ^ bit) for n in range(size)])


def tie(value, *deps):
    return lax.optimization_barrier((value, deps))[0]


def body(layer_in, cotangent, clip_of_frame, w_query, w_key, w_value, w_out, w_up, w_down, norm1_gain, norm1_bias, norm2_gain, norm2_bias):
    seq = lax.axis_size("seq")
    frames = seq // GROUP
    i = lax.axis_index("seq")
    j = lax.axis_index("tp")
    net, core = j // 2, j % 2
    spot, frame = i % GROUP, i // GROUP
    segment, width = layer_in.shape[1], layer_in.shape[3]
    rows = segment * GROUP
    whole = jnp.where(clip_of_frame[0, frames - 1] == 0, 0, 1)
    stream = whole ^ core

    def mine(array, stream):
        return lax.dynamic_slice(array, (net, 0, stream, 0), (1, segment, 1, width)).reshape(segment, width)

    x = mine(layer_in, stream)
    cot = mine(cotangent, stream)
    cot_other = mine(cotangent, 1 - stream)
    clips = lax.dynamic_index_in_dim(clip_of_frame, stream, 0, keepdims=False)
    marks = [lax.dynamic_index_in_dim(clips, frame ^ r, 0, keepdims=False) for r in range(frames)]
    act = jnp.stack([(mark == marks[0]).astype(jnp.int32) for mark in marks])
    sc = jnp.concatenate([jnp.stack([spot ^ j, net, spot, core]).astype(jnp.int32), act[1:]])

    def nets_of(parts, axis):
        packed = jnp.concatenate(parts, axis=axis)
        own = lax.dynamic_index_in_dim(packed, net, 0, keepdims=False)
        other = lax.dynamic_index_in_dim(packed, 1 - net, 0, keepdims=False)
        return own, other

    def across(value):
        return swap(value, "tp", 4, 2)

    def beside(value):
        return swap(value, "tp", 4, 1)

    def to_group(chunks, only=None):
        out = [chunks[0]]
        for k in range(1, GROUP):
            if only is None:
                out.append(swap(chunks[k], "seq", seq, k))
            else:
                pairs = [(n * 4 + t, (n ^ k) * 4 + t) for n in range(seq) for t in only]
                out.append(lax.ppermute(chunks[k], ("seq", "tp"), pairs))
        return out

    def chunks_of(array):
        return [array[k * segment:(k + 1) * segment] for k in range(GROUP)]

    paired = (0, 2) if frames == 2 else (0, 1, 2, 3)

    def cross(value, r):
        pairs = [(n * 4 + t, (n ^ (GROUP * r)) * 4 + t) for n in range(seq) for t in paired]
        return lax.ppermute(value, ("seq", "tp"), pairs)

    xs = to_group([x] * GROUP)
    head_own, head_other = nets_of([w_query, w_key, w_value], 2)
    spots = [(n * 4, n % GROUP) for n in range(seq)]
    unit_y = lax.ppermute(tie(head_other, x), ("seq", "tp"), [(n + p, n + (p ^ 2)) for n, p in spots])
    unit = jnp.where(spot == j, head_own, unit_y)
    unit_c = lax.ppermute(unit, ("seq", "tp"), [(n + q, n + (q ^ 1)) for n, p in spots for q in (p, p ^ 2)])
    rest_own, rest_other = nets_of([w_up, w_down, w_out], 1)
    rest_y = across(tie(rest_other, unit_y))

    qkv, a = call(project_kernel, [((rows, 384), BF), ((rows, width), BF)], sc, [*xs, head_own, unit_y, unit_c, norm1_gain, norm1_bias],
                  scratch=[pltpu.VMEM((width, 384), BF)], us=2, name="k1")
    qb = 256
    kvx = [cross(qkv[:, 128:384], r) for r in range(1, frames)]
    qm, m_own, l_own, acc_own = call(
        lambda *refs: attend_own_kernel(qb, *refs),
        [((2, rows, 128), BF), ((2, rows), F32), ((2, rows), F32), ((128, rows), F32)], act, [qkv],
        scratch=[pltpu.VMEM((128, rows), BF)], us=7, name="own")
    o, ot, lse = call(
        lambda *refs: attend_cross_kernel(qb, *refs),
        [((rows, 128), BF), ((128, rows), F32), ((2, rows), F32)], act, [qm, m_own, l_own, acc_own, *kvx],
        scratch=[pltpu.VMEM((2, rows), F32), pltpu.VMEM((2, rows), F32), pltpu.VMEM((128, rows), F32),
                 pltpu.VMEM((128, rows), BF)], us=7, name="cross")

    os = to_group(chunks_of(o))
    head_y = across(tied('head_y', head_other, rest_y))
    rest = [rest_own, beside(tied('rest_c', rest_own, m_own)), rest_y, beside(tied('rest_yc', rest_y, o))]
    do4, lout, keep, send, dy, gains2 = call(
        middle_kernel,
        [((GROUP, segment, 128), BF), ((segment, width), BF), ((segment, ALL), BF), ((segment, ALL), BF),
         ((segment, width), F32), ((2, width), F32)],
        sc, [x, cot, *os, *rest, norm2_gain, norm2_bias],
        scratch=[pltpu.VMEM((4, 128, width), BF), pltpu.VMEM((4, segment, 128), BF)], us=8, name="mid")
    dos = to_group([do4[k] for k in range(GROUP)])

    (chip,) = call(
        grads_kernel, [((GROUP, 2, ROWS, 512), BF)], sc, [keep, beside(send), cot, cot_other],
        scratch=[pltpu.VMEM((2 * segment, ALL), BF), pltpu.VMEM((2 * segment, width), BF)], us=4, name="grads")

    def add(*terms):
        total = terms[0].astype(F32)
        for term in terms[1:]:
            total = total + term.astype(F32)
        return total.astype(BF)

    def over_frames(value, *deps):
        bit = GROUP
        while bit < seq:
            value = add(value, tie(swap(value, "seq", seq, bit), *deps))
            bit *= 2
        return value

    def add_group(parts, *deps):
        return add(parts[0], *[tie(part, *deps) for part in parts[1:]])

    head_c = beside(tie(head_own, o))
    head_yc = beside(tie(head_y, chip))
    head = [head_own, head_c, head_y, head_yc]
    group = to_group([chip[k] for k in range(GROUP)])
    back = call(
        lambda *refs: back_cross_kernel(qb, frames, *refs),
        [((rows, 256), BF)] * (frames - 1) + [((2, rows, 128), BF), ((2, rows), F32), ((128, rows), F32)],
        tie(act, chip, head_c, head_y), [*dos, qm, ot, lse, *kvx],
        scratch=[pltpu.VMEM((128, rows), BF), pltpu.VMEM((rows, 128), F32), pltpu.VMEM((rows, 128), F32)], us=8, name="bx")
    lout_y = across(tied("lo_y", lout, chip))
    dkv_x, (dom, delta, dqt) = back[:frames - 1], back[frames - 1:]
    dkv_far = [cross(dkv_x[r - 1], r) for r in range(1, frames)]
    dq, dkv_own = call(
        lambda *refs: back_own_kernel(qb, *refs),
        [((rows, 128), BF), ((rows, 256), F32)], tie(act, group[1], group[2], dqt, head_yc, lout_y), [qkv, qm, dom, lse, delta, dqt],
        scratch=[pltpu.VMEM((128, rows), F32), pltpu.VMEM((128, rows), BF), pltpu.VMEM((rows, 128), F32),
                 pltpu.VMEM((rows, 128), F32)], us=8, name="bo")
    total = dkv_own
    for far in dkv_far:
        total = total + far.astype(F32)
    dqkv = jnp.concatenate([dq, total.astype(BF)], axis=1)

    keep_c, send_c = call(grads_heads_kernel, [((width // 2, 384), BF)] * 2, sc, [a, dqkv], us=2, name="kc")
    sum_c = add(keep_c, beside(send_c))
    ds = to_group(chunks_of(tied('ds_c', dqkv, sum_c)))

    def spread(own, far, own_c, far_c):
        out = []
        for n in range(2):
            near = net == n
            mine_n = jnp.where(near, own, far)
            other_n = jnp.where(near, own_c, far_c)
            out.append(jnp.stack([jnp.where(stream == s, mine_n, other_n) for s in range(2)], axis=1))
        return jnp.stack(out)

    layer_out = spread(lout, lout_y, beside(tied("lo_c", lout, dkv_own)), beside(tied("lo_yc", lout_y, dkv_own)))

    got_c = swap(sum_c, "seq", seq, GROUP)
    mine = add(group[0], *[tied("mine", part, sum_c) for part in group[1:]])
    got_0 = swap(mine[0], "seq", seq, GROUP)
    cross_y = across(mine[1])

    gin, gains = call(
        input_kernel, [((segment, width), BF), ((RGAIN, width), F32)],
        tied("k5_lo", tied("k5_c", tied("k5_m", sc, mine), got_c), layer_out), [x, dy, *ds, *head, norm1_gain, norm1_bias, gains2],
        scratch=[pltpu.VMEM((4, width, 384), BF)], us=2, name="k5")
    sum_c = add(sum_c, got_c)
    bit = 2 * GROUP
    while bit < seq:
        sum_c = add(sum_c, swap(sum_c, "seq", seq, bit))
        bit *= 2
    all_c = to_group([sum_c] * GROUP)
    gains = over_frames(gains.astype(BF))
    net_0 = add(mine[0], tied("n0_c", got_0, gains, cross_y, *all_c[1:]))
    bit = 2 * GROUP
    while bit < seq:
        net_0 = add(net_0, swap(net_0, "seq", seq, bit))
        bit *= 2
    all_0 = to_group([jnp.concatenate([net_0, gains])] * GROUP)
    got_1 = swap(tied("n1_a", cross_y, net_0), "seq", seq, GROUP)

    def shard(number):
        pick = spot ^ number
        return jnp.where(pick == 0, all_c[0], jnp.where(pick == 1, all_c[1], jnp.where(pick == 2, all_c[2], all_c[3])))

    far_c = across(jnp.stack([shard(j ^ 2), shard(j ^ 3)]))
    mine_c = jnp.stack([shard(j), far_c[0]])
    other_c = beside(jnp.stack([shard(j ^ 1), far_c[1]]))
    net_1 = add(cross_y, tied("n1_0", got_1, other_c, *all_0[1:]))
    bit = 2 * GROUP
    while bit < seq:
        net_1 = add(net_1, swap(net_1, "seq", seq, bit))
        bit *= 2
    all_1 = to_group([net_1] * GROUP)
    gin = tied("gin_1", gin, net_1)
    gin_y = across(gin)
    input_grad = spread(gin, gin_y, beside(tied("gin_c", gin, gin_y)), beside(gin_y))
    gains = sum(part[ROWS:].astype(F32) for part in all_0)
    gains = tied("gains_1", gains, net_1)
    gains = gains + beside(gains)
    gains_y = across(gains)
    gains = jnp.stack([jnp.where(net == n, gains, gains_y) for n in range(2)])
    gq, gk, gv = call(unpack_heads_kernel, [((2, 512, 128), F32)] * 3, sc, [mine_c, other_c], us=1, name="uc")
    up, down, out = call(
        unpack_kernel, [((2, 512, 512), F32), ((2, 512, 512), F32), ((2, 128, 512), F32)],
        tie(sc, gq, input_grad, gains), [*all_0, *all_1], us=3, name="up")
    return (layer_out, input_grad, gq, gk, gv, out, up, down, gains[:, 0], gains[:, 1], gains[:, 2], gains[:, 3])


def solution(mesh):
    tokens = P(None, "seq", None, None)
    columns = P(None, None, "tp")
    rows = P(None, "tp", None)
    return jax.shard_map(
        body,
        mesh=mesh,
        in_specs=(tokens, tokens, P(), columns, columns, columns, rows, columns, rows, P(), P(), P(), P()),
        out_specs=(tokens, tokens, columns, columns, columns, rows, columns, rows, P(), P(), P(), P()),
        check_vma=False,
    )
```

```python
import math

import jax
import jax.numpy as jnp
from jax import lax
from jax.experimental import pallas as pl
from jax.experimental.pallas import tpu as pltpu
from jax.sharding import PartitionSpec as P

HEAD_DIM = 64
EPS = 1e-05
BF = jnp.bfloat16
F32 = jnp.float32
VMEM_LIMIT = 50 * 1024 * 1024
OPT = {"scale": 10}


def tied(name, value, *deps, default=1):
    return tie(value, *deps) if OPT.get(name, default) else value


GROUP = 4
RUP, RDOWN, ROUT = 128, 128, 32
ROWS = RUP + RDOWN + ROUT
DU_AT, H_AT, B_AT, DZ_AT, O_AT, ALL = 0, 1024, 2048, 2560, 3072, 3328
RGAIN = 16
C_GELU = math.sqrt(2.0 / math.pi)


def dot(a, b, ca=1, cb=0):
    return lax.dot_general(a, b, (((ca,), (cb,)), ((), ())), preferred_element_type=F32)


def norm_parts(v):
    center = v - jnp.mean(v, axis=-1, keepdims=True)
    inv = lax.rsqrt(jnp.mean(center * center, axis=-1, keepdims=True) + EPS)
    return center * inv, inv


def norm_back(dout, hat, inv, gain):
    e = dout * gain
    mean_e = jnp.mean(e, axis=-1, keepdims=True)
    mean_eh = jnp.mean(e * hat, axis=-1, keepdims=True)
    return (e - mean_e - hat * mean_eh) * inv


def vspec():
    return pl.BlockSpec(memory_space=pltpu.VMEM)


def sspec():
    return pl.BlockSpec(memory_space=pltpu.SMEM)


def call(kernel, outs, scalars, args, scratch=(), us=1.0, name=None, after=()):
    us = OPT.get('us_' + name, us) if name else us
    count = len(args) + 1

    def run(*refs):
        kernel(*refs[:count], *refs[count + len(after):])

    return pl.pallas_call(
        run,
        out_shape=[jax.ShapeDtypeStruct(s, d) for s, d in outs],
        in_specs=[sspec()] + [vspec()] * len(args) + [pl.BlockSpec(memory_space=pl.ANY)] * len(after),
        out_specs=[vspec()] * len(outs),
        scratch_shapes=list(scratch),
        compiler_params=pltpu.CompilerParams(vmem_limit_bytes=VMEM_LIMIT),
        cost_estimate=pl.CostEstimate(flops=int(us * 1.1e9 * OPT.get("scale", 1)), bytes_accessed=0, transcendentals=0),
    )(scalars, *args, *after)


def pick_shard(sc, wo, wy, wc, w_s):
    for e, ref in enumerate((wo, wc, wy, wc)):
        @pl.when(sc[0] == e)
        def _(ref=ref):
            w_s[...] = ref[...]


def project_kernel(sc, x0, x1, x2, x3, wo, wy, wc, gain, bias, qkv, a_out, w_s):
    pick_shard(sc, wo, wy, wc, w_s)
    g = gain[pl.ds(sc[1], 1), :]
    b = bias[pl.ds(sc[1], 1), :]
    for k, ref in enumerate((x0, x1, x2, x3)):
        hat, _ = norm_parts(ref[...].astype(F32))
        a = (hat * g + b).astype(BF)
        out = dot(a, w_s[...])
        rows = pl.ds(k * ref.shape[0], ref.shape[0])
        a_out[rows, :] = a
        qkv[rows, 0:128] = (out[:, 0:128].astype(BF).astype(F32) * (1.0 / math.sqrt(HEAD_DIM))).astype(BF)
        qkv[rows, 128:384] = out[:, 128:384].astype(BF)


def attend_block(k, vt, qm, m_s, l_s, acc, qb, first):
    n = qm.shape[1]
    for h in range(2):
        rows = slice(h * HEAD_DIM, (h + 1) * HEAD_DIM)

        def block(b, _, h=h, rows=rows):
            cols = pl.ds(pl.multiple_of(b * qb, qb), qb)
            st = dot(k, qm[h, cols, :], 1, 1)
            m = jnp.max(st, axis=0, keepdims=True)
            if not first:
                old = m_s[h:h + 1, cols]
                m = jnp.maximum(old, m)
            pt = jnp.exp(st - m)
            total = jnp.sum(pt, axis=0, keepdims=True)
            new = dot(vt[rows, :], pt.astype(BF))
            if not first:
                fix = jnp.exp(old - m)
                total = total + l_s[h:h + 1, cols] * fix
                new = new + acc[rows, cols] * fix
            m_s[h:h + 1, cols] = m
            l_s[h:h + 1, cols] = total
            acc[rows, cols] = new
            return 0

        lax.fori_loop(0, n // qb, block, 0)


def split_heads(value, dst):
    lane = lax.broadcasted_iota(jnp.int32, value.shape, 1)
    zero = jnp.zeros_like(value)
    dst[0] = jnp.where(lane < HEAD_DIM, value, zero)
    dst[1] = jnp.where(lane < HEAD_DIM, zero, value)


def attend_own_kernel(qb, act, qkv, qm, m_s, l_s, acc, vt):
    split_heads(qkv[:, 0:128], qm)
    vt[...] = qkv[:, 256:384].T
    attend_block(qkv[:, 128:256], vt, qm, m_s, l_s, acc, qb, True)


def attend_cross_kernel(qb, act, qm, m_in, l_in, acc_in, *refs):
    kvx = refs[:-7]
    o_out, ot_out, lse_out, m_s, l_s, acc, vt = refs[-7:]
    m_s[...] = m_in[...]
    l_s[...] = l_in[...]
    acc[...] = acc_in[...]
    for r, kv in enumerate(kvx):
        @pl.when(act[r + 1] != 0)
        def _(kv=kv):
            vt[...] = kv[:, 128:256].T
            attend_block(kv[:, 0:128], vt, qm, m_s, l_s, acc, qb, False)
    for h in range(2):
        rows = slice(h * HEAD_DIM, (h + 1) * HEAD_DIM)
        ot_out[rows, :] = acc[rows, :] / l_s[h:h + 1, :]
        lse_out[h:h + 1, :] = m_s[h:h + 1, :] + jnp.log(l_s[h:h + 1, :])
    o_out[...] = ot_out[...].T.astype(BF)


def back_block(k, v, qm, dom, lse, delta, kt, dk_s, dv_s, dqt, qb):
    kt[...] = k.T
    dk_s[...] = jnp.zeros_like(dk_s)
    dv_s[...] = jnp.zeros_like(dv_s)
    n = qm.shape[1]
    for h in range(2):
        rows = slice(h * HEAD_DIM, (h + 1) * HEAD_DIM)

        def block(b, _, h=h, rows=rows):
            cols = pl.ds(pl.multiple_of(b * qb, qb), qb)
            qh = qm[h, cols, :]
            dh = dom[h, cols, :]
            pt = jnp.exp(dot(k, qh, 1, 1) - lse[h:h + 1, cols])
            dv_s[...] += dot(pt.astype(BF), dh)
            dst = (pt * (dot(v, dh, 1, 1) - delta[h:h + 1, cols])).astype(BF)
            dk_s[...] += dot(dst, qh)
            dqt[rows, cols] += dot(kt[rows, :], dst)
            return 0

        lax.fori_loop(0, n // qb, block, 0)


def back_cross_kernel(qb, frames, act, d0, d1, d2, d3, qm, ot, lse, *refs):
    kvx, refs = refs[:frames - 1], refs[frames - 1:]
    dkv_x, (dom, delta, dqt, kt, dk_s, dv_s) = refs[:frames - 1], refs[frames - 1:]
    seg = d0.shape[0]
    for k, ref in enumerate((d0, d1, d2, d3)):
        cols = slice(k * seg, (k + 1) * seg)
        d = ref[...]
        split_heads(d, dom.at[:, cols, :])
        dt = d.astype(F32).T * ot[:, cols]
        for h in range(2):
            delta[h:h + 1, cols] = jnp.sum(dt[h * HEAD_DIM:(h + 1) * HEAD_DIM, :], axis=0, keepdims=True)
    dqt[...] = jnp.zeros_like(dqt)
    for r in range(frames - 1):
        @pl.when(act[r + 1] != 0)
        def _(r=r):
            back_block(kvx[r][:, 0:128], kvx[r][:, 128:256], qm, dom, lse, delta, kt, dk_s, dv_s, dqt, qb)
            dkv_x[r][:, 0:128] = dk_s[...].astype(BF)
            dkv_x[r][:, 128:256] = dv_s[...].astype(BF)

        @pl.when(act[r + 1] == 0)
        def _(r=r):
            dkv_x[r][...] = jnp.zeros_like(dkv_x[r])


def back_own_kernel(qb, act, qkv, qm, dom, lse, delta, dqt_in, dq_out, dkv_own, dqt, kt, dk_s, dv_s):
    dqt[...] = dqt_in[...]
    back_block(qkv[:, 128:256], qkv[:, 256:384], qm, dom, lse, delta, kt, dk_s, dv_s, dqt, qb)
    dkv_own[:, 0:128] = dk_s[...]
    dkv_own[:, 128:256] = dv_s[...]
    dq_out[...] = (dqt[...].T * (1.0 / math.sqrt(HEAD_DIM))).astype(BF)


def gelu_parts(u):
    t = jnp.tanh(C_GELU * (u + 0.044715 * (u * u * u)))
    value = 0.5 * u * (1.0 + t)
    slope = 0.5 * (1.0 + t) + 0.5 * u * (1.0 - t * t) * (C_GELU * (1.0 + 3 * 0.044715 * (u * u)))
    return value, slope


def middle_kernel(sc, x, g, o0, o1, o2, o3, w0, w1, w2, w3, gain, bias, do_out, lout, keep, send, dy_out, gains, wo_s, o_s):
    mats = (w0, w1, w2, w3)
    for e in range(4):
        wo_s[e] = mats[e][1024:1152, :]
    gain_row = gain[pl.ds(sc[1], 1), :]
    mid = x[...].astype(F32)
    for k, ref in enumerate((o0, o1, o2, o3)):
        o_s[k] = ref[...]
        mid = mid + dot(ref[...], wo_s[sc[0] ^ k])
    hat, inv = norm_parts(mid)
    b = (hat * gain_row + bias[pl.ds(sc[1], 1), :]).astype(BF)
    cot = g[...]
    dy_out[...] = mid
    db = jnp.zeros_like(mid)
    for e in range(4):
        up = mats[e][0:512, :]
        down = mats[e][512:1024, :]
        value, slope = gelu_parts(dot(b, up))
        h = value.astype(BF)
        pack, spot = (keep, send)[e % 2], 512 * (e // 2)
        pack[:, H_AT + spot:H_AT + spot + 512] = h
        dy_out[...] += dot(h, down)
        du = (dot(cot, down, 1, 1) * slope).astype(BF)
        pack[:, DU_AT + spot:DU_AT + spot + 512] = du
        db = db + dot(du, up, 1, 1)
    lout[...] = dy_out[...].astype(BF)
    gains[0:1, :] = jnp.sum(db * hat, axis=0, keepdims=True)
    gains[1:2, :] = jnp.sum(db, axis=0, keepdims=True)
    dy = cot.astype(F32) + norm_back(db, hat, inv, gain_row)
    dy_out[...] = dy
    dz = dy.astype(BF)
    for e in range(4):
        pack, spot = (keep, send)[e % 2], 128 * (e // 2)
        pack[:, O_AT + spot:O_AT + spot + 128] = o_s[sc[0] ^ e]
    for pack in (keep, send):
        pack[:, B_AT:B_AT + 512] = b
        pack[:, DZ_AT:DZ_AT + 512] = dz
    for k in range(4):
        do_out[k] = dot(dz, wo_s[sc[0] ^ k], 1, 1).astype(BF)


def store_pieces(dst, e, row, value, rows, sc):
    for a in range(GROUP):
        dst[a ^ sc[2], e, row:row + rows, :] = value[a * rows:(a + 1) * rows, :]


def grads_kernel(sc, mine, other, g_mine, g_other, out, both, g):
    n = mine.shape[0]
    both[0:n, :] = mine[...]
    both[n:2 * n, :] = other[...]
    g[0:n, :] = g_mine[...]
    g[n:2 * n, :] = g_other[...]
    for e in range(2):
        du = both[:, DU_AT + 512 * e:DU_AT + 512 * e + 512]
        h = both[:, H_AT + 512 * e:H_AT + 512 * e + 512]
        o = both[:, O_AT + 128 * e:O_AT + 128 * e + 128]
        store_pieces(out, e, 0, dot(both[:, B_AT:B_AT + 512], du, 0, 0).astype(BF), RUP, sc)
        store_pieces(out, e, RUP, dot(h, g[...], 0, 0).astype(BF), RDOWN, sc)
        store_pieces(out, e, RUP + RDOWN, dot(o, both[:, DZ_AT:DZ_AT + 512], 0, 0).astype(BF), ROUT, sc)


def grads_heads_kernel(sc, a, dqkv, keep, send):
    grad = dot(a[...], dqkv[...], 0, 0).astype(BF)
    size = grad.shape[0] // 2
    for n in range(2):
        @pl.when(sc[3] == n)
        def _(n=n):
            keep[...] = grad[n * size:(n + 1) * size, :]
            send[...] = grad[(1 - n) * size:(2 - n) * size, :]


def input_kernel(sc, x, dy, d0, d1, d2, d3, w0, w1, w2, w3, gain, bias, gains2, gin, gains, w_s):
    mats = (w0, w1, w2, w3)
    for e in range(4):
        w_s[e] = mats[e][...]
    gain_row = gain[pl.ds(sc[1], 1), :]
    hat, inv = norm_parts(x[...].astype(F32))
    da = jnp.zeros_like(hat)
    for k, ref in enumerate((d0, d1, d2, d3)):
        da = da + dot(ref[...], w_s[sc[0] ^ k], 1, 1)
    gin[...] = (dy[...] + norm_back(da, hat, inv, gain_row)).astype(BF)
    gains[...] = jnp.zeros_like(gains)
    gains[0:1, :] = jnp.sum(da * hat, axis=0, keepdims=True)
    gains[1:2, :] = jnp.sum(da, axis=0, keepdims=True)
    gains[2:4, :] = gains2[...]


def unpack_kernel(sc, p0, p1, p2, p3, q0, q1, q2, q3, up, down, out):
    for rel, parts in enumerate(((p0, p1, p2, p3), (q0, q1, q2, q3))):
        net = sc[1] ^ rel
        for k, src in enumerate(parts):
            a = k ^ sc[2]
            up[net, pl.ds(pl.multiple_of(a * RUP, RUP), RUP), :] = src[0:RUP, :].astype(F32)
            down[net, pl.ds(pl.multiple_of(a * RDOWN, RDOWN), RDOWN), :] = src[RUP:RUP + RDOWN, :].astype(F32)
            out[net, pl.ds(pl.multiple_of(a * ROUT, ROUT), ROUT), :] = src[RUP + RDOWN:ROWS, :].astype(F32)

def unpack_heads_kernel(sc, mine, other, q, k, v):
    size = mine.shape[1]
    for rel in range(2):
        net = sc[1] ^ rel
        for core, src in enumerate((mine, other)):
            rows = pl.ds(pl.multiple_of((core ^ sc[3]) * size, size), size)
            q[net, rows, :] = src[rel, :, 0:128].astype(F32)
            k[net, rows, :] = src[rel, :, 128:256].astype(F32)
            v[net, rows, :] = src[rel, :, 256:384].astype(F32)


def swap(value, axis, size, bit):
    return lax.ppermute(value, axis, [(n, n ^ bit) for n in range(size)])


def tie(value, *deps):
    return lax.optimization_barrier((value, deps))[0]


def body(layer_in, cotangent, clip_of_frame, w_query, w_key, w_value, w_out, w_up, w_down, norm1_gain, norm1_bias, norm2_gain, norm2_bias):
    seq = lax.axis_size("seq")
    frames = seq // GROUP
    i = lax.axis_index("seq")
    j = lax.axis_index("tp")
    net, core = j // 2, j % 2
    spot, frame = i % GROUP, i // GROUP
    segment, width = layer_in.shape[1], layer_in.shape[3]
    rows = segment * GROUP
    whole = jnp.where(clip_of_frame[0, frames - 1] == 0, 0, 1)
    stream = whole ^ core

    def mine(array, stream):
        return lax.dynamic_slice(array, (net, 0, stream, 0), (1, segment, 1, width)).reshape(segment, width)

    x = mine(layer_in, stream)
    cot = mine(cotangent, stream)
    cot_other = mine(cotangent, 1 - stream)
    clips = lax.dynamic_index_in_dim(clip_of_frame, stream, 0, keepdims=False)
    marks = [lax.dynamic_index_in_dim(clips, frame ^ r, 0, keepdims=False) for r in range(frames)]
    act = jnp.stack([(mark == marks[0]).astype(jnp.int32) for mark in marks])
    sc = jnp.concatenate([jnp.stack([spot ^ j, net, spot, core]).astype(jnp.int32), act[1:]])

    def nets_of(parts, axis):
        packed = jnp.concatenate(parts, axis=axis)
        own = lax.dynamic_index_in_dim(packed, net, 0, keepdims=False)
        other = lax.dynamic_index_in_dim(packed, 1 - net, 0, keepdims=False)
        return own, other

    def across(value):
        return swap(value, "tp", 4, 2)

    def beside(value):
        return swap(value, "tp", 4, 1)

    def to_group(chunks, only=None):
        out = [chunks[0]]
        for k in range(1, GROUP):
            if only is None:
                out.append(swap(chunks[k], "seq", seq, k))
            else:
                pairs = [(n * 4 + t, (n ^ k) * 4 + t) for n in range(seq) for t in only]
                out.append(lax.ppermute(chunks[k], ("seq", "tp"), pairs))
        return out

    def chunks_of(array):
        return [array[k * segment:(k + 1) * segment] for k in range(GROUP)]

    paired = (0, 2) if frames == 2 else (0, 1, 2, 3)

    def cross(value, r):
        pairs = [(n * 4 + t, (n ^ (GROUP * r)) * 4 + t) for n in range(seq) for t in paired]
        return lax.ppermute(value, ("seq", "tp"), pairs)

    xs = to_group([x] * GROUP)
    head_own, head_other = nets_of([w_query, w_key, w_value], 2)
    spots = [(n * 4, n % GROUP) for n in range(seq)]
    unit_y = lax.ppermute(tie(head_other, x), ("seq", "tp"), [(n + p, n + (p ^ 2)) for n, p in spots])
    unit = jnp.where(spot == j, head_own, unit_y)
    unit_c = lax.ppermute(unit, ("seq", "tp"), [(n + q, n + (q ^ 1)) for n, p in spots for q in (p, p ^ 2)])
    rest_own, rest_other = nets_of([w_up, w_down, w_out], 1)
    rest_y = across(tie(rest_other, unit_y))

    qkv, a = call(project_kernel, [((rows, 384), BF), ((rows, width), BF)], sc, [*xs, head_own, unit_y, unit_c, norm1_gain, norm1_bias],
                  scratch=[pltpu.VMEM((width, 384), BF)], us=2, name="k1")
    qb = 1024
    kvx = [cross(qkv[:, 128:384], r) for r in range(1, frames)]
    qm, m_own, l_own, acc_own = call(
        lambda *refs: attend_own_kernel(qb, *refs),
        [((2, rows, 128), BF), ((2, rows), F32), ((2, rows), F32), ((128, rows), F32)], act, [qkv],
        scratch=[pltpu.VMEM((128, rows), BF)], us=7, name="own")
    o, ot, lse = call(
        lambda *refs: attend_cross_kernel(qb, *refs),
        [((rows, 128), BF), ((128, rows), F32), ((2, rows), F32)], act, [qm, m_own, l_own, acc_own, *kvx],
        scratch=[pltpu.VMEM((2, rows), F32), pltpu.VMEM((2, rows), F32), pltpu.VMEM((128, rows), F32),
                 pltpu.VMEM((128, rows), BF)], us=7, name="cross")

    os = to_group(chunks_of(o))
    head_y = across(tied('head_y', head_other, rest_y))
    rest = [rest_own, beside(tied('rest_c', rest_own, m_own)), rest_y, beside(tied('rest_yc', rest_y, o))]
    do4, lout, keep, send, dy, gains2 = call(
        middle_kernel,
        [((GROUP, segment, 128), BF), ((segment, width), BF), ((segment, ALL), BF), ((segment, ALL), BF),
         ((segment, width), F32), ((2, width), F32)],
        sc, [x, cot, *os, *rest, norm2_gain, norm2_bias],
        scratch=[pltpu.VMEM((4, 128, width), BF), pltpu.VMEM((4, segment, 128), BF)], us=8, name="mid")
    dos = to_group([do4[k] for k in range(GROUP)])

    (chip,) = call(
        grads_kernel, [((GROUP, 2, ROWS, 512), BF)], sc, [keep, beside(send), cot, cot_other],
        scratch=[pltpu.VMEM((2 * segment, ALL), BF), pltpu.VMEM((2 * segment, width), BF)], us=4, name="grads")

    def add(*terms):
        total = terms[0].astype(F32)
        for term in terms[1:]:
            total = total + term.astype(F32)
        return total.astype(BF)

    def over_frames(value, *deps):
        bit = GROUP
        while bit < seq:
            value = add(value, tie(swap(value, "seq", seq, bit), *deps))
            bit *= 2
        return value

    def add_group(parts, *deps):
        return add(parts[0], *[tie(part, *deps) for part in parts[1:]])

    head_c = beside(tie(head_own, o))
    head_yc = beside(tie(head_y, chip))
    head = [head_own, head_c, head_y, head_yc]
    group = to_group([chip[k] for k in range(GROUP)])
    back = call(
        lambda *refs: back_cross_kernel(qb, frames, *refs),
        [((rows, 256), BF)] * (frames - 1) + [((2, rows, 128), BF), ((2, rows), F32), ((128, rows), F32)],
        tie(act, chip, head_c, head_y), [*dos, qm, ot, lse, *kvx],
        scratch=[pltpu.VMEM((128, rows), BF), pltpu.VMEM((rows, 128), F32), pltpu.VMEM((rows, 128), F32)], us=8, name="bx")
    lout_y = across(tied("lo_y", lout, chip))
    dkv_x, (dom, delta, dqt) = back[:frames - 1], back[frames - 1:]
    dkv_far = [cross(dkv_x[r - 1], r) for r in range(1, frames)]
    dq, dkv_own = call(
        lambda *refs: back_own_kernel(qb, *refs),
        [((rows, 128), BF), ((rows, 256), F32)], tie(act, group[1], group[2], dqt, head_yc, lout_y), [qkv, qm, dom, lse, delta, dqt],
        scratch=[pltpu.VMEM((128, rows), F32), pltpu.VMEM((128, rows), BF), pltpu.VMEM((rows, 128), F32),
                 pltpu.VMEM((rows, 128), F32)], us=8, name="bo")
    total = dkv_own
    for far in dkv_far:
        total = total + far.astype(F32)
    dqkv = jnp.concatenate([dq, total.astype(BF)], axis=1)

    keep_c, send_c = call(grads_heads_kernel, [((width // 2, 384), BF)] * 2, sc, [a, dqkv], us=2, name="kc")
    sum_c = add(keep_c, beside(send_c))
    ds = to_group(chunks_of(tied('ds_c', dqkv, sum_c)))

    def spread(own, far, own_c, far_c):
        out = []
        for n in range(2):
            near = net == n
            mine_n = jnp.where(near, own, far)
            other_n = jnp.where(near, own_c, far_c)
            out.append(jnp.stack([jnp.where(stream == s, mine_n, other_n) for s in range(2)], axis=1))
        return jnp.stack(out)

    layer_out = spread(lout, lout_y, beside(tied("lo_c", lout, dkv_own)), beside(tied("lo_yc", lout_y, dkv_own)))

    got_c = swap(sum_c, "seq", seq, GROUP)
    mine = add(group[0], *[tied("mine", part, sum_c) for part in group[1:]])
    got_0 = swap(mine[0], "seq", seq, GROUP)
    cross_y = across(mine[1])

    gin, gains = call(
        input_kernel, [((segment, width), BF), ((RGAIN, width), F32)],
        tied("k5_lo", tied("k5_c", tied("k5_m", sc, mine), got_c), layer_out), [x, dy, *ds, *head, norm1_gain, norm1_bias, gains2],
        scratch=[pltpu.VMEM((4, width, 384), BF)], us=2, name="k5")
    sum_c = add(sum_c, got_c)
    bit = 2 * GROUP
    while bit < seq:
        sum_c = add(sum_c, swap(sum_c, "seq", seq, bit))
        bit *= 2
    all_c = to_group([sum_c] * GROUP)
    gains = over_frames(gains.astype(BF))
    net_0 = add(mine[0], tied("n0_c", got_0, gains, cross_y, *all_c[1:]))
    bit = 2 * GROUP
    while bit < seq:
        net_0 = add(net_0, swap(net_0, "seq", seq, bit))
        bit *= 2
    all_0 = to_group([jnp.concatenate([net_0, gains])] * GROUP)
    got_1 = swap(tied("n1_a", cross_y, net_0), "seq", seq, GROUP)

    def shard(number):
        pick = spot ^ number
        return jnp.where(pick == 0, all_c[0], jnp.where(pick == 1, all_c[1], jnp.where(pick == 2, all_c[2], all_c[3])))

    far_c = across(jnp.stack([shard(j ^ 2), shard(j ^ 3)]))
    mine_c = jnp.stack([shard(j), far_c[0]])
    other_c = beside(jnp.stack([shard(j ^ 1), far_c[1]]))
    net_1 = add(cross_y, tied("n1_0", got_1, other_c, *all_0[1:]))
    bit = 2 * GROUP
    while bit < seq:
        net_1 = add(net_1, swap(net_1, "seq", seq, bit))
        bit *= 2
    all_1 = to_group([net_1] * GROUP)
    gin = tied("gin_1", gin, net_1)
    gin_y = across(gin)
    input_grad = spread(gin, gin_y, beside(tied("gin_c", gin, gin_y)), beside(gin_y))
    gains = sum(part[ROWS:].astype(F32) for part in all_0)
    gains = tied("gains_1", gains, net_1)
    gains = gains + beside(gains)
    gains_y = across(gains)
    gains = jnp.stack([jnp.where(net == n, gains, gains_y) for n in range(2)])
    gq, gk, gv = call(unpack_heads_kernel, [((2, 512, 128), F32)] * 3, sc, [mine_c, other_c], us=1, name="uc")
    up, down, out = call(
        unpack_kernel, [((2, 512, 512), F32), ((2, 512, 512), F32), ((2, 128, 512), F32)],
        tie(sc, gq, input_grad, gains), [*all_0, *all_1], us=3, name="up")
    return (layer_out, input_grad, gq, gk, gv, out, up, down, gains[:, 0], gains[:, 1], gains[:, 2], gains[:, 3])


def solution(mesh):
    tokens = P(None, "seq", None, None)
    columns = P(None, None, "tp")
    rows = P(None, "tp", None)
    return jax.shard_map(
        body,
        mesh=mesh,
        in_specs=(tokens, tokens, P(), columns, columns, columns, rows, columns, rows, P(), P(), P(), P()),
        out_specs=(tokens, tokens, columns, columns, columns, rows, columns, rows, P(), P(), P(), P()),
        check_vma=False,
    )
```

```python
import math

import jax
import jax.numpy as jnp
from jax import lax
from jax.experimental import pallas as pl
from jax.experimental.pallas import tpu as pltpu
from jax.sharding import PartitionSpec as P

HEAD_DIM = 64
EPS = 1e-05
BF = jnp.bfloat16
F32 = jnp.float32
VMEM_LIMIT = 50 * 1024 * 1024
OPT = {"scale": 10}


def tied(name, value, *deps, default=1):
    return tie(value, *deps) if OPT.get(name, default) else value


GROUP = 4
RUP, RDOWN, ROUT = 128, 128, 32
ROWS = RUP + RDOWN + ROUT
DU_AT, H_AT, B_AT, DZ_AT, O_AT, ALL = 0, 1024, 2048, 2560, 3072, 3328
RGAIN = 16
C_GELU = math.sqrt(2.0 / math.pi)


def dot(a, b, ca=1, cb=0):
    return lax.dot_general(a, b, (((ca,), (cb,)), ((), ())), preferred_element_type=F32)


def norm_parts(v):
    center = v - jnp.mean(v, axis=-1, keepdims=True)
    inv = lax.rsqrt(jnp.mean(center * center, axis=-1, keepdims=True) + EPS)
    return center * inv, inv


def norm_back(dout, hat, inv, gain):
    e = dout * gain
    mean_e = jnp.mean(e, axis=-1, keepdims=True)
    mean_eh = jnp.mean(e * hat, axis=-1, keepdims=True)
    return (e - mean_e - hat * mean_eh) * inv


def vspec():
    return pl.BlockSpec(memory_space=pltpu.VMEM)


def sspec():
    return pl.BlockSpec(memory_space=pltpu.SMEM)


def call(kernel, outs, scalars, args, scratch=(), us=1.0, name=None, after=()):
    us = OPT.get('us_' + name, us) if name else us
    count = len(args) + 1

    def run(*refs):
        kernel(*refs[:count], *refs[count + len(after):])

    return pl.pallas_call(
        run,
        out_shape=[jax.ShapeDtypeStruct(s, d) for s, d in outs],
        in_specs=[sspec()] + [vspec()] * len(args) + [pl.BlockSpec(memory_space=pl.ANY)] * len(after),
        out_specs=[vspec()] * len(outs),
        scratch_shapes=list(scratch),
        compiler_params=pltpu.CompilerParams(vmem_limit_bytes=VMEM_LIMIT),
        cost_estimate=pl.CostEstimate(flops=int(us * 1.1e9 * OPT.get("scale", 1)), bytes_accessed=0, transcendentals=0),
    )(scalars, *args, *after)


def pick_shard(sc, wo, wy, wc, w_s):
    for e, ref in enumerate((wo, wc, wy, wc)):
        @pl.when(sc[0] == e)
        def _(ref=ref):
            w_s[...] = ref[...]


def project_kernel(sc, x0, x1, x2, x3, wo, wy, wc, gain, bias, qkv, a_out, w_s):
    pick_shard(sc, wo, wy, wc, w_s)
    g = gain[pl.ds(sc[1], 1), :]
    b = bias[pl.ds(sc[1], 1), :]
    for k, ref in enumerate((x0, x1, x2, x3)):
        hat, _ = norm_parts(ref[...].astype(F32))
        a = (hat * g + b).astype(BF)
        out = dot(a, w_s[...])
        rows = pl.ds(k * ref.shape[0], ref.shape[0])
        a_out[rows, :] = a
        qkv[rows, 0:128] = (out[:, 0:128].astype(BF).astype(F32) * (1.0 / math.sqrt(HEAD_DIM))).astype(BF)
        qkv[rows, 128:384] = out[:, 128:384].astype(BF)


def attend_block(k, vt, qm, m_s, l_s, acc, qb, first):
    def head(h, _):
        rows = pl.ds(pl.multiple_of(h * HEAD_DIM, HEAD_DIM), HEAD_DIM)
        row = pl.ds(h, 1)
        st = dot(k, qm[h], 1, 1)
        m = jnp.max(st, axis=0, keepdims=True)
        if not first:
            old = m_s[row, :]
            m = jnp.maximum(old, m)
        pt = jnp.exp(st - m)
        total = jnp.sum(pt, axis=0, keepdims=True)
        new = dot(vt[rows, :], pt.astype(BF))
        if not first:
            fix = jnp.exp(old - m)
            total = total + l_s[row, :] * fix
            new = new + acc[rows, :] * fix
        m_s[row, :] = m
        l_s[row, :] = total
        acc[rows, :] = new
        return 0

    lax.fori_loop(0, 2, head, 0)


def split_heads(value, dst):
    lane = lax.broadcasted_iota(jnp.int32, value.shape, 1)
    zero = jnp.zeros_like(value)
    dst[0] = jnp.where(lane < HEAD_DIM, value, zero)
    dst[1] = jnp.where(lane < HEAD_DIM, zero, value)


def attend_own_kernel(qb, act, qkv, qm, m_s, l_s, acc, vt):
    split_heads(qkv[:, 0:128], qm)
    vt[...] = qkv[:, 256:384].T
    attend_block(qkv[:, 128:256], vt, qm, m_s, l_s, acc, qb, True)


def attend_cross_kernel(qb, act, qm, m_in, l_in, acc_in, *refs):
    kvx = refs[:-7]
    o_out, ot_out, lse_out, m_s, l_s, acc, vt = refs[-7:]
    m_s[...] = m_in[...]
    l_s[...] = l_in[...]
    acc[...] = acc_in[...]
    for r, kv in enumerate(kvx):
        @pl.when(act[r + 1] != 0)
        def _(kv=kv):
            vt[...] = kv[:, 128:256].T
            attend_block(kv[:, 0:128], vt, qm, m_s, l_s, acc, qb, False)
    for h in range(2):
        rows = slice(h * HEAD_DIM, (h + 1) * HEAD_DIM)
        ot_out[rows, :] = acc[rows, :] / l_s[h:h + 1, :]
        lse_out[h:h + 1, :] = m_s[h:h + 1, :] + jnp.log(l_s[h:h + 1, :])
    o_out[...] = ot_out[...].T.astype(BF)


def back_block(k, v, qm, dom, lse, delta, kt, dk_s, dv_s, dqt, qb):
    kt[...] = k.T
    dk_s[...] = jnp.zeros_like(dk_s)
    dv_s[...] = jnp.zeros_like(dv_s)

    def head(h, _):
        rows = pl.ds(pl.multiple_of(h * HEAD_DIM, HEAD_DIM), HEAD_DIM)
        row = pl.ds(h, 1)
        qh = qm[h]
        dh = dom[h]
        pt = jnp.exp(dot(k, qh, 1, 1) - lse[row, :])
        dv_s[...] += dot(pt.astype(BF), dh)
        dst = (pt * (dot(v, dh, 1, 1) - delta[row, :])).astype(BF)
        dk_s[...] += dot(dst, qh)
        dqt[rows, :] += dot(kt[rows, :], dst)
        return 0

    lax.fori_loop(0, 2, head, 0)


def back_cross_kernel(qb, frames, act, d0, d1, d2, d3, qm, ot, lse, *refs):
    kvx, refs = refs[:frames - 1], refs[frames - 1:]
    dkv_x, (dom, delta, dqt, kt, dk_s, dv_s) = refs[:frames - 1], refs[frames - 1:]
    seg = d0.shape[0]
    for k, ref in enumerate((d0, d1, d2, d3)):
        cols = slice(k * seg, (k + 1) * seg)
        d = ref[...]
        split_heads(d, dom.at[:, cols, :])
        dt = d.astype(F32).T * ot[:, cols]
        for h in range(2):
            delta[h:h + 1, cols] = jnp.sum(dt[h * HEAD_DIM:(h + 1) * HEAD_DIM, :], axis=0, keepdims=True)
    dqt[...] = jnp.zeros_like(dqt)
    for r in range(frames - 1):
        @pl.when(act[r + 1] != 0)
        def _(r=r):
            back_block(kvx[r][:, 0:128], kvx[r][:, 128:256], qm, dom, lse, delta, kt, dk_s, dv_s, dqt, qb)
            dkv_x[r][:, 0:128] = dk_s[...].astype(BF)
            dkv_x[r][:, 128:256] = dv_s[...].astype(BF)

        @pl.when(act[r + 1] == 0)
        def _(r=r):
            dkv_x[r][...] = jnp.zeros_like(dkv_x[r])


def back_own_kernel(qb, act, qkv, qm, dom, lse, delta, dqt_in, dq_out, dkv_own, dqt, kt, dk_s, dv_s):
    dqt[...] = dqt_in[...]
    back_block(qkv[:, 128:256], qkv[:, 256:384], qm, dom, lse, delta, kt, dk_s, dv_s, dqt, qb)
    dkv_own[:, 0:128] = dk_s[...]
    dkv_own[:, 128:256] = dv_s[...]
    dq_out[...] = (dqt[...].T * (1.0 / math.sqrt(HEAD_DIM))).astype(BF)


def gelu_parts(u):
    t = jnp.tanh(C_GELU * (u + 0.044715 * (u * u * u)))
    value = 0.5 * u * (1.0 + t)
    slope = 0.5 * (1.0 + t) + 0.5 * u * (1.0 - t * t) * (C_GELU * (1.0 + 3 * 0.044715 * (u * u)))
    return value, slope


def middle_kernel(sc, x, g, o0, o1, o2, o3, w0, w1, w2, w3, gain, bias, do_out, lout, keep, send, dy_out, gains, wo_s, o_s):
    mats = (w0, w1, w2, w3)
    for e in range(4):
        wo_s[e] = mats[e][1024:1152, :]
    gain_row = gain[pl.ds(sc[1], 1), :]
    mid = x[...].astype(F32)
    for k, ref in enumerate((o0, o1, o2, o3)):
        o_s[k] = ref[...]
        mid = mid + dot(ref[...], wo_s[sc[0] ^ k])
    hat, inv = norm_parts(mid)
    b = (hat * gain_row + bias[pl.ds(sc[1], 1), :]).astype(BF)
    cot = g[...]
    dy_out[...] = mid
    db = jnp.zeros_like(mid)
    for e in range(4):
        up = mats[e][0:512, :]
        down = mats[e][512:1024, :]
        value, slope = gelu_parts(dot(b, up))
        h = value.astype(BF)
        pack, spot = (keep, send)[e % 2], 512 * (e // 2)
        pack[:, H_AT + spot:H_AT + spot + 512] = h
        dy_out[...] += dot(h, down)
        du = (dot(cot, down, 1, 1) * slope).astype(BF)
        pack[:, DU_AT + spot:DU_AT + spot + 512] = du
        db = db + dot(du, up, 1, 1)
    lout[...] = dy_out[...].astype(BF)
    gains[0:1, :] = jnp.sum(db * hat, axis=0, keepdims=True)
    gains[1:2, :] = jnp.sum(db, axis=0, keepdims=True)
    dy = cot.astype(F32) + norm_back(db, hat, inv, gain_row)
    dy_out[...] = dy
    dz = dy.astype(BF)
    for e in range(4):
        pack, spot = (keep, send)[e % 2], 128 * (e // 2)
        pack[:, O_AT + spot:O_AT + spot + 128] = o_s[sc[0] ^ e]
    for pack in (keep, send):
        pack[:, B_AT:B_AT + 512] = b
        pack[:, DZ_AT:DZ_AT + 512] = dz
    for k in range(4):
        do_out[k] = dot(dz, wo_s[sc[0] ^ k], 1, 1).astype(BF)


def store_pieces(dst, e, row, value, rows, sc):
    for a in range(GROUP):
        dst[a ^ sc[2], e, row:row + rows, :] = value[a * rows:(a + 1) * rows, :]


def grads_kernel(sc, mine, other, g_mine, g_other, out, both, g):
    n = mine.shape[0]
    both[0:n, :] = mine[...]
    both[n:2 * n, :] = other[...]
    g[0:n, :] = g_mine[...]
    g[n:2 * n, :] = g_other[...]
    for e in range(2):
        du = both[:, DU_AT + 512 * e:DU_AT + 512 * e + 512]
        h = both[:, H_AT + 512 * e:H_AT + 512 * e + 512]
        o = both[:, O_AT + 128 * e:O_AT + 128 * e + 128]
        store_pieces(out, e, 0, dot(both[:, B_AT:B_AT + 512], du, 0, 0).astype(BF), RUP, sc)
        store_pieces(out, e, RUP, dot(h, g[...], 0, 0).astype(BF), RDOWN, sc)
        store_pieces(out, e, RUP + RDOWN, dot(o, both[:, DZ_AT:DZ_AT + 512], 0, 0).astype(BF), ROUT, sc)


def grads_heads_kernel(sc, a, dqkv, keep, send):
    grad = dot(a[...], dqkv[...], 0, 0).astype(BF)
    size = grad.shape[0] // 2
    for n in range(2):
        @pl.when(sc[3] == n)
        def _(n=n):
            keep[...] = grad[n * size:(n + 1) * size, :]
            send[...] = grad[(1 - n) * size:(2 - n) * size, :]


def input_kernel(sc, x, dy, d0, d1, d2, d3, w0, w1, w2, w3, gain, bias, gains2, gin, gains, w_s):
    mats = (w0, w1, w2, w3)
    for e in range(4):
        w_s[e] = mats[e][...]
    gain_row = gain[pl.ds(sc[1], 1), :]
    hat, inv = norm_parts(x[...].astype(F32))
    da = jnp.zeros_like(hat)
    for k, ref in enumerate((d0, d1, d2, d3)):
        da = da + dot(ref[...], w_s[sc[0] ^ k], 1, 1)
    gin[...] = (dy[...] + norm_back(da, hat, inv, gain_row)).astype(BF)
    gains[...] = jnp.zeros_like(gains)
    gains[0:1, :] = jnp.sum(da * hat, axis=0, keepdims=True)
    gains[1:2, :] = jnp.sum(da, axis=0, keepdims=True)
    gains[2:4, :] = gains2[...]


def unpack_kernel(sc, p0, p1, p2, p3, q0, q1, q2, q3, up, down, out):
    for rel, parts in enumerate(((p0, p1, p2, p3), (q0, q1, q2, q3))):
        net = sc[1] ^ rel
        for k, src in enumerate(parts):
            a = k ^ sc[2]
            up[net, pl.ds(pl.multiple_of(a * RUP, RUP), RUP), :] = src[0:RUP, :].astype(F32)
            down[net, pl.ds(pl.multiple_of(a * RDOWN, RDOWN), RDOWN), :] = src[RUP:RUP + RDOWN, :].astype(F32)
            out[net, pl.ds(pl.multiple_of(a * ROUT, ROUT), ROUT), :] = src[RUP + RDOWN:ROWS, :].astype(F32)

def unpack_heads_kernel(sc, mine, other, q, k, v):
    size = mine.shape[1]
    for rel in range(2):
        net = sc[1] ^ rel
        for core, src in enumerate((mine, other)):
            rows = pl.ds(pl.multiple_of((core ^ sc[3]) * size, size), size)
            q[net, rows, :] = src[rel, :, 0:128].astype(F32)
            k[net, rows, :] = src[rel, :, 128:256].astype(F32)
            v[net, rows, :] = src[rel, :, 256:384].astype(F32)


def swap(value, axis, size, bit):
    return lax.ppermute(value, axis, [(n, n ^ bit) for n in range(size)])


def tie(value, *deps):
    return lax.optimization_barrier((value, deps))[0]


def body(layer_in, cotangent, clip_of_frame, w_query, w_key, w_value, w_out, w_up, w_down, norm1_gain, norm1_bias, norm2_gain, norm2_bias):
    seq = lax.axis_size("seq")
    frames = seq // GROUP
    i = lax.axis_index("seq")
    j = lax.axis_index("tp")
    net, core = j // 2, j % 2
    spot, frame = i % GROUP, i // GROUP
    segment, width = layer_in.shape[1], layer_in.shape[3]
    rows = segment * GROUP
    whole = jnp.where(clip_of_frame[0, frames - 1] == 0, 0, 1)
    stream = whole ^ core

    def mine(array, stream):
        return lax.dynamic_slice(array, (net, 0, stream, 0), (1, segment, 1, width)).reshape(segment, width)

    x = mine(layer_in, stream)
    cot = mine(cotangent, stream)
    cot_other = mine(cotangent, 1 - stream)
    clips = lax.dynamic_index_in_dim(clip_of_frame, stream, 0, keepdims=False)
    marks = [lax.dynamic_index_in_dim(clips, frame ^ r, 0, keepdims=False) for r in range(frames)]
    act = jnp.stack([(mark == marks[0]).astype(jnp.int32) for mark in marks])
    sc = jnp.concatenate([jnp.stack([spot ^ j, net, spot, core]).astype(jnp.int32), act[1:]])

    def nets_of(parts, axis):
        packed = jnp.concatenate(parts, axis=axis)
        own = lax.dynamic_index_in_dim(packed, net, 0, keepdims=False)
        other = lax.dynamic_index_in_dim(packed, 1 - net, 0, keepdims=False)
        return own, other

    def across(value):
        return swap(value, "tp", 4, 2)

    def beside(value):
        return swap(value, "tp", 4, 1)

    def to_group(chunks, only=None):
        out = [chunks[0]]
        for k in range(1, GROUP):
            if only is None:
                out.append(swap(chunks[k], "seq", seq, k))
            else:
                pairs = [(n * 4 + t, (n ^ k) * 4 + t) for n in range(seq) for t in only]
                out.append(lax.ppermute(chunks[k], ("seq", "tp"), pairs))
        return out

    def chunks_of(array):
        return [array[k * segment:(k + 1) * segment] for k in range(GROUP)]

    paired = (0, 2) if frames == 2 else (0, 1, 2, 3)

    def cross(value, r):
        pairs = [(n * 4 + t, (n ^ (GROUP * r)) * 4 + t) for n in range(seq) for t in paired]
        return lax.ppermute(value, ("seq", "tp"), pairs)

    xs = to_group([x] * GROUP)
    head_own, head_other = nets_of([w_query, w_key, w_value], 2)
    spots = [(n * 4, n % GROUP) for n in range(seq)]
    unit_y = lax.ppermute(tie(head_other, x), ("seq", "tp"), [(n + p, n + (p ^ 2)) for n, p in spots])
    unit = jnp.where(spot == j, head_own, unit_y)
    unit_c = lax.ppermute(unit, ("seq", "tp"), [(n + q, n + (q ^ 1)) for n, p in spots for q in (p, p ^ 2)])
    rest_own, rest_other = nets_of([w_up, w_down, w_out], 1)
    rest_y = across(tie(rest_other, unit_y))

    qkv, a = call(project_kernel, [((rows, 384), BF), ((rows, width), BF)], sc, [*xs, head_own, unit_y, unit_c, norm1_gain, norm1_bias],
                  scratch=[pltpu.VMEM((width, 384), BF)], us=2, name="k1")
    qb = 1024
    kvx = [cross(qkv[:, 128:384], r) for r in range(1, frames)]
    qm, m_own, l_own, acc_own = call(
        lambda *refs: attend_own_kernel(qb, *refs),
        [((2, rows, 128), BF), ((2, rows), F32), ((2, rows), F32), ((128, rows), F32)], act, [qkv],
        scratch=[pltpu.VMEM((128, rows), BF)], us=7, name="own")
    o, ot, lse = call(
        lambda *refs: attend_cross_kernel(qb, *refs),
        [((rows, 128), BF), ((128, rows), F32), ((2, rows), F32)], act, [qm, m_own, l_own, acc_own, *kvx],
        scratch=[pltpu.VMEM((2, rows), F32), pltpu.VMEM((2, rows), F32), pltpu.VMEM((128, rows), F32),
                 pltpu.VMEM((128, rows), BF)], us=7, name="cross")

    os = to_group(chunks_of(o))
    head_y = across(tied('head_y', head_other, rest_y))
    rest = [rest_own, beside(tied('rest_c', rest_own, m_own)), rest_y, beside(tied('rest_yc', rest_y, o))]
    do4, lout, keep, send, dy, gains2 = call(
        middle_kernel,
        [((GROUP, segment, 128), BF), ((segment, width), BF), ((segment, ALL), BF), ((segment, ALL), BF),
         ((segment, width), F32), ((2, width), F32)],
        sc, [x, cot, *os, *rest, norm2_gain, norm2_bias],
        scratch=[pltpu.VMEM((4, 128, width), BF), pltpu.VMEM((4, segment, 128), BF)], us=8, name="mid")
    dos = to_group([do4[k] for k in range(GROUP)])

    (chip,) = call(
        grads_kernel, [((GROUP, 2, ROWS, 512), BF)], sc, [keep, beside(send), cot, cot_other],
        scratch=[pltpu.VMEM((2 * segment, ALL), BF), pltpu.VMEM((2 * segment, width), BF)], us=4, name="grads")

    def add(*terms):
        total = terms[0].astype(F32)
        for term in terms[1:]:
            total = total + term.astype(F32)
        return total.astype(BF)

    def over_frames(value, *deps):
        bit = GROUP
        while bit < seq:
            value = add(value, tie(swap(value, "seq", seq, bit), *deps))
            bit *= 2
        return value

    def add_group(parts, *deps):
        return add(parts[0], *[tie(part, *deps) for part in parts[1:]])

    head_c = beside(tie(head_own, o))
    head_yc = beside(tie(head_y, chip))
    head = [head_own, head_c, head_y, head_yc]
    group = to_group([chip[k] for k in range(GROUP)])
    back = call(
        lambda *refs: back_cross_kernel(qb, frames, *refs),
        [((rows, 256), BF)] * (frames - 1) + [((2, rows, 128), BF), ((2, rows), F32), ((128, rows), F32)],
        tie(act, chip, head_c, head_y), [*dos, qm, ot, lse, *kvx],
        scratch=[pltpu.VMEM((128, rows), BF), pltpu.VMEM((rows, 128), F32), pltpu.VMEM((rows, 128), F32)], us=8, name="bx")
    lout_y = across(tied("lo_y", lout, chip))
    dkv_x, (dom, delta, dqt) = back[:frames - 1], back[frames - 1:]
    dkv_far = [cross(dkv_x[r - 1], r) for r in range(1, frames)]
    dq, dkv_own = call(
        lambda *refs: back_own_kernel(qb, *refs),
        [((rows, 128), BF), ((rows, 256), F32)], tie(act, group[1], group[2], dqt, head_yc, lout_y), [qkv, qm, dom, lse, delta, dqt],
        scratch=[pltpu.VMEM((128, rows), F32), pltpu.VMEM((128, rows), BF), pltpu.VMEM((rows, 128), F32),
                 pltpu.VMEM((rows, 128), F32)], us=8, name="bo")
    total = dkv_own
    for far in dkv_far:
        total = total + far.astype(F32)
    dqkv = jnp.concatenate([dq, total.astype(BF)], axis=1)

    keep_c, send_c = call(grads_heads_kernel, [((width // 2, 384), BF)] * 2, sc, [a, dqkv], us=2, name="kc")
    sum_c = add(keep_c, beside(send_c))
    ds = to_group(chunks_of(tied('ds_c', dqkv, sum_c)))

    def spread(own, far, own_c, far_c):
        out = []
        for n in range(2):
            near = net == n
            mine_n = jnp.where(near, own, far)
            other_n = jnp.where(near, own_c, far_c)
            out.append(jnp.stack([jnp.where(stream == s, mine_n, other_n) for s in range(2)], axis=1))
        return jnp.stack(out)

    layer_out = spread(lout, lout_y, beside(tied("lo_c", lout, dkv_own)), beside(tied("lo_yc", lout_y, dkv_own)))

    got_c = swap(sum_c, "seq", seq, GROUP)
    mine = add(group[0], *[tied("mine", part, sum_c) for part in group[1:]])
    got_0 = swap(mine[0], "seq", seq, GROUP)
    cross_y = across(mine[1])

    gin, gains = call(
        input_kernel, [((segment, width), BF), ((RGAIN, width), F32)],
        tied("k5_lo", tied("k5_c", tied("k5_m", sc, mine), got_c), layer_out), [x, dy, *ds, *head, norm1_gain, norm1_bias, gains2],
        scratch=[pltpu.VMEM((4, width, 384), BF)], us=2, name="k5")
    sum_c = add(sum_c, got_c)
    bit = 2 * GROUP
    while bit < seq:
        sum_c = add(sum_c, swap(sum_c, "seq", seq, bit))
        bit *= 2
    all_c = to_group([sum_c] * GROUP)
    gains = over_frames(gains.astype(BF))
    net_0 = add(mine[0], tied("n0_c", got_0, gains, cross_y, *all_c[1:]))
    bit = 2 * GROUP
    while bit < seq:
        net_0 = add(net_0, swap(net_0, "seq", seq, bit))
        bit *= 2
    all_0 = to_group([jnp.concatenate([net_0, gains])] * GROUP)
    got_1 = swap(tied("n1_a", cross_y, net_0), "seq", seq, GROUP)

    def shard(number):
        pick = spot ^ number
        return jnp.where(pick == 0, all_c[0], jnp.where(pick == 1, all_c[1], jnp.where(pick == 2, all_c[2], all_c[3])))

    far_c = across(jnp.stack([shard(j ^ 2), shard(j ^ 3)]))
    mine_c = jnp.stack([shard(j), far_c[0]])
    other_c = beside(jnp.stack([shard(j ^ 1), far_c[1]]))
    net_1 = add(cross_y, tied("n1_0", got_1, other_c, *all_0[1:]))
    bit = 2 * GROUP
    while bit < seq:
        net_1 = add(net_1, swap(net_1, "seq", seq, bit))
        bit *= 2
    all_1 = to_group([net_1] * GROUP)
    gin = tied("gin_1", gin, net_1)
    gin_y = across(gin)
    input_grad = spread(gin, gin_y, beside(tied("gin_c", gin, gin_y)), beside(gin_y))
    gains = sum(part[ROWS:].astype(F32) for part in all_0)
    gains = tied("gains_1", gains, net_1)
    gains = gains + beside(gains)
    gains_y = across(gains)
    gains = jnp.stack([jnp.where(net == n, gains, gains_y) for n in range(2)])
    gq, gk, gv = call(unpack_heads_kernel, [((2, 512, 128), F32)] * 3, sc, [mine_c, other_c], us=1, name="uc")
    up, down, out = call(
        unpack_kernel, [((2, 512, 512), F32), ((2, 512, 512), F32), ((2, 128, 512), F32)],
        tie(sc, gq, input_grad, gains), [*all_0, *all_1], us=3, name="up")
    return (layer_out, input_grad, gq, gk, gv, out, up, down, gains[:, 0], gains[:, 1], gains[:, 2], gains[:, 3])


def solution(mesh):
    tokens = P(None, "seq", None, None)
    columns = P(None, None, "tp")
    rows = P(None, "tp", None)
    return jax.shard_map(
        body,
        mesh=mesh,
        in_specs=(tokens, tokens, P(), columns, columns, columns, rows, columns, rows, P(), P(), P(), P()),
        out_specs=(tokens, tokens, columns, columns, columns, rows, columns, rows, P(), P(), P(), P()),
        check_vma=False,
    )
```
